32 devices in a mesh: row: 8 (over z, y), col: 4 (over x, core).
Axes of the slice: x: 2, y: 2, z: 4, core: 2. Of those that a mesh axis runs over, the one named last changes fastest.
Arguments:
- layer_input: float32 [768, 8192], P('col', 'row'), may hold values from -6 to 6
- ln1_gain: float32 [768], P('col'), may hold values from 0.25 to 1.75
- ln1_bias: float32 [768], P('col'), may hold values from -3 to 3
- w_query: bfloat16 [768, 768], P('row', 'col'), may hold values from -0.21875 to 0.21875
- w_key: bfloat16 [768, 768], P('row', 'col'), may hold values from -0.21875 to 0.21875
- w_value: bfloat16 [768, 768], P('row', 'col'), may hold values from -0.21875 to 0.21875
- b_query: float32 [768], P('col'), may hold values from -3 to 3
- b_value: float32 [768], P('col'), may hold values from -3 to 3
- w_out: bfloat16 [768, 768], P('col', 'row'), may hold values from -2.5 to 2.5
- b_out: float32 [768], P('col'), may hold values from -3 to 3
- ln2_gain: float32 [768], P('col'), may hold values from 0.25 to 1.75
- ln2_bias: float32 [768], P('col'), may hold values from -3 to 3
- w_fc1: bfloat16 [768, 3072], P('row', 'col')
- b_fc1: float32 [3072], P('col'), may hold values from -3 to 3
- w_fc2: bfloat16 [3072, 768], P('col', 'row'), may hold values from -0.109375 to 0.109375
- b_fc2: float32 [768], P('col'), may hold values from -3 to 3
- seq_lengths: int32 [8, 3], P('row'), may hold values from 1 to 1022, as said below
- cotangent: float32 [768, 8192], P('col', 'row'), may hold values from -6 to 6
Outputs:
- output: float32 [768, 8192], P('col', 'row')
- grad_input: float32 [768, 8192], P('col', 'row')
- grad_ln1_gain: float32 [768], P('col')
- grad_ln1_bias: float32 [768], P('col')
- grad_w_query: float32 [768, 768], P('row', 'col')
- grad_w_key: float32 [768, 768], P('row', 'col')
- grad_w_value: float32 [768, 768], P('row', 'col')
- grad_b_query: float32 [768], P('col')
- grad_b_value: float32 [768], P('col')
- grad_w_out: float32 [768, 768], P('col', 'row')
- grad_b_out: float32 [768], P('col')
- grad_ln2_gain: float32 [768], P('col')
- grad_ln2_bias: float32 [768], P('col')
- grad_w_fc1: float32 [768, 3072], P('row', 'col')
- grad_b_fc1: float32 [3072], P('col')
- grad_w_fc2: float32 [3072, 768], P('col', 'row')
- grad_b_fc2: float32 [768], P('col')
The draws below stay inside these ranges and needn't reach their ends.
Inputs may be any that keep to these rules, and one draw needn't show every extreme that they name: `seq_lengths`: row p lists the lengths of the 3 sequences packed in this order into pack p; they sum to at most 1024, and the remaining positions are padding. In every pack the second sequence starts within the first 256 positions and ends within the last 256 positions.
All inputs are finite; a program needn't handle non-finite values.
Results may differ from the reference program's by a relative error of at most 0.017.
Values may be sent and summed in bfloat16 or wider, within the bound.
A program may use at most 128 MiB of HBM per device.

```python
import jax
import jax.numpy as jnp
from jax import lax

D = 768
HEADS = 12
HEAD_DIM = 64
FF = 3072
TOK_DEV = 1024
PACKS = 8
TOKENS = 8192
Q_ROWS = 256


def draw_seq_lengths(key, part):
    key = jax.random.fold_in(key, 11)
    first_key, long_key, last_key = jax.random.split(key, 3)
    leading = jax.random.randint(first_key, (PACKS,), 1, Q_ROWS)
    spanning = jax.random.randint(long_key, (PACKS,), TOK_DEV - Q_ROWS - leading + 1, TOK_DEV - leading)
    trailing = jax.random.randint(last_key, (PACKS,), 1, TOK_DEV - leading - spanning + 1)
    fullest = jnp.arange(PACKS) == 0
    leading = jnp.where(fullest, 1, leading)
    spanning = jnp.where(fullest, TOK_DEV - 2, spanning)
    trailing = jnp.where(fullest, 1, trailing)
    return jnp.stack([leading, spanning, trailing], axis=1).astype(jnp.int32)


def draw_w_fc1(key, part):
    key = jax.random.fold_in(key, 23)
    noise_key, common_key = jax.random.split(key)
    noise = jax.random.truncated_normal(noise_key, -4.0, 4.0, (D, FF), jnp.float32)
    common = jax.random.truncated_normal(common_key, -3.0, 3.0, (FF,), jnp.float32)
    return ((noise + common[None, :]) * (2.0 * D) ** (-0.5)).astype(jnp.bfloat16)


def block_scale(rng, shape, pieces, low, top_value):
    loudness = 1.0
    for dim, parts in pieces:
        heights = jax.random.uniform(jax.random.fold_in(jax.random.fold_in(rng, 6), dim), (parts,), jnp.float32, low / len(pieces), top_value / len(pieces))
        loudness = loudness * jnp.repeat(jnp.exp(heights), shape[dim] // parts).reshape((-1,) + (1,) * (len(shape) - 1 - dim))
    return loudness


def centred(key, shape, scale, limit, shards=(), kind=jnp.bfloat16):
    gain = block_scale(key, shape, shards, -0.22, 0.18) if shards else 1.0
    result = jax.random.normal(key, shape, jnp.float32) * scale * gain
    return jnp.minimum(jnp.maximum(result, -limit), limit).astype(kind)


def setup_inputs(seed: int = 0) -> dict:
    streams_of = jax.random.split(jax.random.key(seed), 19)
    layer_input = centred(streams_of[0], (D, TOKENS), 1.0, 6.0, ((0, 4), (1, 8)), jnp.float32)
    ln1_gain = jnp.clip(1.0 + 0.15 * jax.random.normal(streams_of[1], (D,), jnp.float32), 0.25, 1.75)
    ln1_bias = centred(streams_of[2], (D,), 0.5, 3.0, ((0, 4),), jnp.float32)
    w_query = centred(streams_of[3], (D, D), D ** -0.5, 0.21875, ((0, 8), (1, 4)))
    w_key = centred(streams_of[4], (D, D), D ** -0.5, 0.21875, ((0, 8), (1, 4)))
    w_value = centred(streams_of[5], (D, D), D ** -0.5, 0.21875, ((0, 8), (1, 4)))
    b_query = centred(streams_of[6], (D,), 0.5, 3.0, ((0, 4),), jnp.float32)
    b_value = centred(streams_of[7], (D,), 0.5, 3.0, ((0, 4),), jnp.float32)
    w_out = centred(streams_of[8], (D, D), (max(1, D // 128)) ** -0.5, 2.5, ((0, 4), (1, 8)))
    b_out = centred(streams_of[9], (D,), 0.5, 3.0, ((0, 4),), jnp.float32)
    ln2_gain = jnp.clip(1.0 + 0.15 * jax.random.normal(streams_of[10], (D,), jnp.float32), 0.25, 1.75)
    ln2_bias = centred(streams_of[11], (D,), 0.5, 3.0, ((0, 4),), jnp.float32)
    w_fc1 = draw_w_fc1(jax.random.fold_in(streams_of[18], 71), 0)
    b_fc1 = centred(streams_of[13], (FF,), 0.5, 3.0, ((0, 4),), jnp.float32)
    w_fc2 = centred(streams_of[14], (FF, D), FF ** -0.5, 0.109375, ((0, 4), (1, 8)))
    b_fc2 = centred(streams_of[15], (D,), 0.5, 3.0, ((0, 4),), jnp.float32)
    seq_lengths = draw_seq_lengths(jax.random.fold_in(streams_of[18], 71), 0)
    cotangent = centred(streams_of[17], (D, TOKENS), 1.0, 6.0, ((0, 4), (1, 8)), jnp.float32)
    return dict(layer_input=layer_input, ln1_gain=ln1_gain, ln1_bias=ln1_bias, w_query=w_query, w_key=w_key, w_value=w_value, b_query=b_query, b_value=b_value, w_out=w_out, b_out=b_out, ln2_gain=ln2_gain, ln2_bias=ln2_bias, w_fc1=w_fc1, b_fc1=b_fc1, w_fc2=w_fc2, b_fc2=b_fc2, seq_lengths=seq_lengths, cotangent=cotangent)


EPS = 1e-05
NEG = -1e+30
PRECISE = lax.Precision.HIGHEST

@jax.custom_vjp
def low(v):
    return lax.optimization_barrier(v.astype(jnp.bfloat16)).astype(jnp.float32)

@jax.custom_vjp
def low_back(v):
    return v

def low_keep(v):
    return (low(v), None)

def low_pass(kept, grad):
    return (grad,)

def back_keep(v):
    return (v, None)

def back_low(kept, grad):
    return (low(grad),)
low.defvjp(low_keep, low_pass)
low_back.defvjp(back_keep, back_low)

def product(first_op, second_op):
    return jnp.dot(first_op, second_op, precision=PRECISE, preferred_element_type=jnp.float32)

def smooth_gate(values):
    return jax.nn.gelu(values, approximate=True)

def normalize(values, norm_gain, norm_shift):
    row_mean = lax.optimization_barrier(jnp.mean(values, axis=1, keepdims=True))
    centered = values - row_mean
    variance = lax.optimization_barrier(jnp.mean(centered * centered, axis=1, keepdims=True))
    return centered * lax.rsqrt(variance + EPS) * norm_gain + norm_shift

def attend(queries, key_rows, value_rows, segment):
    length = queries.shape[0]
    heads_q = queries.reshape(length, HEADS, HEAD_DIM)
    heads_k = key_rows.reshape(length, HEADS, HEAD_DIM)
    heads_v = value_rows.reshape(length, HEADS, HEAD_DIM)
    scores = jnp.einsum('qhd,khd->hqk', heads_q, heads_k, precision=PRECISE)
    scores = low_back(scores)
    places = jnp.arange(length, dtype=jnp.int32)
    allowed = (segment[:, None] == segment[None, :]) & (places[None, :] <= places[:, None])
    scores = jnp.where(allowed[None], scores, NEG)
    row_top = lax.optimization_barrier(jnp.max(scores, axis=2, keepdims=True))
    expo_vals = jnp.exp(scores - row_top)
    attn_probs = low(expo_vals / lax.optimization_barrier(jnp.sum(expo_vals, axis=2, keepdims=True)))
    mixed = jnp.einsum('hqk,khd->qhd', attn_probs, heads_v, precision=PRECISE)
    return mixed.reshape(length, HEADS * HEAD_DIM)

def pack_layer(params, pack_rows, segment):
    ln1_gain, ln1_bias, w_query, w_key, w_value, b_query, b_value, w_out, b_out, ln2_gain, ln2_bias, w_fc1, b_fc1, w_fc2, b_fc2 = params
    scaling = HEAD_DIM ** (-0.5)
    normed1 = low(normalize(pack_rows, ln1_gain, ln1_bias))
    queries = low(low_back((product(normed1, w_query) + b_query) * scaling))
    key_rows = low(low_back(product(normed1, w_key)))
    value_rows = low(low_back(product(normed1, w_value) + b_value))
    mixed = low(low_back(attend(queries, key_rows, value_rows, segment)))
    middle = pack_rows + low_back(product(mixed, w_out) + b_out)
    normed2 = low(normalize(middle, ln2_gain, ln2_bias))
    hidden = low(smooth_gate(low_back(product(normed2, w_fc1) + b_fc1)))
    return middle + low_back(product(hidden, w_fc2) + b_fc2)

def reference(layer_input, ln1_gain, ln1_bias, w_query, w_key, w_value, b_query, b_value, w_out, b_out, ln2_gain, ln2_bias, w_fc1, b_fc1, w_fc2, b_fc2, seq_lengths, cotangent):
    params = tuple((item.astype(jnp.float32) for item in (ln1_gain, ln1_bias, w_query, w_key, w_value, b_query, b_value, w_out, b_out, ln2_gain, ln2_bias, w_fc1, b_fc1, w_fc2, b_fc2)))
    seq_ends = jnp.cumsum(seq_lengths, axis=1).astype(jnp.int32)
    places = jnp.arange(TOK_DEV, dtype=jnp.int32)
    segments = lax.optimization_barrier(jnp.sum((places[None, :, None] >= seq_ends[:, None, :]).astype(jnp.int32), axis=2)).astype(jnp.int32)

    def whole_layer(inputs_all, weights_all):

        def one_pack(item):
            return pack_layer(weights_all, item[0], item[1])
        outputs = lax.map(jax.checkpoint(one_pack), (inputs_all.reshape(PACKS, TOK_DEV, D), segments))
        return outputs.reshape(TOKENS, D)
    output, pull = jax.vjp(whole_layer, layer_input.astype(jnp.float32).T, params)
    grad_input, grads = pull(cotangent.astype(jnp.float32).T)
    return (output.T, grad_input.T, grads[0], grads[1], grads[2], grads[3], grads[4], grads[5], grads[6], grads[7], grads[8], grads[9], grads[10], grads[11], grads[12], grads[13], grads[14])
```

```python
import functools

import jax
import jax.numpy as jnp
from jax import lax
from jax.experimental import pallas as pl
from jax.experimental.pallas import tpu as pltpu
from jax.sharding import PartitionSpec as P

HEADS = 12
HEAD_DIM = 64


EPS = 1e-05
NEG = -1e30


def to_half(values):
    return values.astype(jnp.bfloat16)


def product(first_op, second_op):
    return jnp.dot(first_op, second_op, preferred_element_type=jnp.float32)


def product_left(first_op, second_op):
    return lax.dot_general(
        first_op, second_op, (((0,), (0,)), ((), ())), preferred_element_type=jnp.float32
    )


def product_right(first_op, second_op):
    return lax.dot_general(
        first_op, second_op, (((1,), (1,)), ((), ())), preferred_element_type=jnp.float32
    )


def column_sum(values):
    return jnp.sum(values.astype(jnp.float32), axis=0)


def smooth_gate(values):
    return jax.nn.gelu(values, approximate=True)


def query_positions(pack_rows):
    col_count = lax.axis_size("col")
    col_index = lax.axis_index("col")
    share_rows = pack_rows // col_count
    return col_index * share_rows + jnp.arange(share_rows, dtype=jnp.int32)


def feature_rows(block_rows):
    return lax.all_gather(block_rows, "col", axis=1, tiled=True)


def feature_sums(partial_value):
    return lax.psum_scatter(partial_value, "col", scatter_dimension=1, tiled=True)


def to_heads(block_rows):
    return lax.all_to_all(block_rows, "col", split_axis=0, concat_axis=1, tiled=True)


def to_features(block_rows):
    spread = lax.all_to_all(block_rows, "col", split_axis=1, concat_axis=0, tiled=True)
    return spread


def norm_forward(block_rows, norm_gain, norm_shift):
    local_width = block_rows.shape[1]
    full_width = local_width * lax.axis_size("col")
    row_sums, row_squares = lax.psum(
        (jnp.sum(block_rows, axis=1), jnp.sum(block_rows * block_rows, axis=1)), "col"
    )
    row_mean = (row_sums / full_width)[:, None]
    variance = (row_squares / full_width)[:, None] - row_mean * row_mean
    row_scale = lax.rsqrt(variance + EPS)
    scaled = (block_rows - row_mean) * row_scale
    normed = feature_rows(to_half(scaled * norm_gain + norm_shift))
    return (normed, scaled, row_scale)


def norm_backward(upstream, scaled, row_scale, norm_gain):
    full_width = upstream.shape[1] * lax.axis_size("col")
    weighted = upstream * norm_gain
    row_sums, row_along = lax.psum(
        (jnp.sum(weighted, axis=1), jnp.sum(weighted * scaled, axis=1)), "col"
    )
    grad_rows = row_scale * (
        weighted - (row_sums / full_width)[:, None] - scaled * (row_along / full_width)[:, None]
    )
    return (grad_rows, jnp.sum(upstream * scaled, axis=0), jnp.sum(upstream, axis=0))


def split_heads(block_rows):
    return block_rows.reshape(block_rows.shape[0], HEADS, HEAD_DIM)


def masked_scores(queries, all_keys, query_pos, segment):
    scores = jnp.einsum(
        "qhd,khd->hqk",
        split_heads(queries),
        split_heads(all_keys),
        preferred_element_type=jnp.float32,
    )
    key_pos = jnp.arange(all_keys.shape[0], dtype=jnp.int32)
    allowed = (segment[query_pos][:, None] == segment[None, :]) & (
        key_pos[None, :] <= query_pos[:, None]
    )
    return jnp.where(allowed[None], scores, NEG)


def attention_forward(queries, all_keys, all_values, query_pos, segment):
    scores = masked_scores(queries, all_keys, query_pos, segment)
    row_top = jnp.max(scores, axis=2, keepdims=True)
    expo_vals = jnp.exp(scores - row_top)
    row_total = jnp.sum(expo_vals, axis=2, keepdims=True)
    attn_probs = to_half(expo_vals / row_total)
    mixed = jnp.einsum(
        "hqk,khd->qhd", attn_probs, split_heads(all_values), preferred_element_type=jnp.float32
    )
    return (mixed.reshape(queries.shape[0], -1), row_top + jnp.log(row_total))


def attention_backward(queries, all_keys, all_values, query_pos, segment, log_total, grad_mixed):
    scores = masked_scores(queries, all_keys, query_pos, segment)
    attn_probs = jnp.exp(scores - log_total)
    grad_heads = split_heads(grad_mixed)
    grad_probs = jnp.einsum(
        "qhd,khd->hqk", grad_heads, split_heads(all_values), preferred_element_type=jnp.float32
    )
    row_inner = jnp.sum(attn_probs * grad_probs, axis=2, keepdims=True)
    grad_scores = to_half(attn_probs * (grad_probs - row_inner))
    grad_queries = jnp.einsum(
        "hqk,khd->qhd", grad_scores, split_heads(all_keys), preferred_element_type=jnp.float32
    )
    grad_keys = jnp.einsum(
        "hqk,qhd->khd", grad_scores, split_heads(queries), preferred_element_type=jnp.float32
    )
    grad_values = jnp.einsum(
        "hqk,qhd->khd", to_half(attn_probs), grad_heads, preferred_element_type=jnp.float32
    )
    key_count = all_keys.shape[0]
    return (
        grad_queries.reshape(queries.shape[0], -1),
        grad_keys.reshape(key_count, -1),
        grad_values.reshape(key_count, -1),
    )


def shards(
    layer_input,
    ln1_gain,
    ln1_bias,
    w_query,
    w_key,
    w_value,
    b_query,
    b_value,
    w_out,
    b_out,
    ln2_gain,
    ln2_bias,
    w_fc1,
    b_fc1,
    w_fc2,
    b_fc2,
    seq_lengths,
    cotangent,
):
    scaling = HEAD_DIM ** (-0.5)
    input_rows = layer_input.T
    cotangent_rows = cotangent.T
    pack_rows = input_rows.shape[0]
    seq_ends = jnp.cumsum(seq_lengths[0])
    places = jnp.arange(pack_rows, dtype=jnp.int32)
    segment = jnp.sum((places[:, None] >= seq_ends[None, :]).astype(jnp.int32), axis=1)
    query_pos = query_positions(pack_rows)
    gathered = (
        lax.all_gather(w_query, "row", axis=0, tiled=True),
        lax.all_gather(w_key, "row", axis=0, tiled=True),
        lax.all_gather(w_value, "row", axis=0, tiled=True),
        lax.all_gather(w_fc1, "row", axis=0, tiled=True),
        lax.all_gather(w_out.T, "row", axis=0, tiled=True),
        lax.all_gather(w_fc2.T, "row", axis=0, tiled=True),
    )
    full_query, full_key, full_value, full_fc1, full_out, full_fc2 = gathered
    normed1, scaled1, scale1 = norm_forward(input_rows, ln1_gain, ln1_bias)
    query_part = to_half((product(normed1, full_query) + b_query) * scaling)
    key_part = to_half(product(normed1, full_key))
    value_part = to_half(product(normed1, full_value) + b_value)
    queries = to_heads(query_part)
    all_keys, all_values = (
        lax.all_gather(key_part, "col", axis=1, tiled=True),
        lax.all_gather(value_part, "col", axis=1, tiled=True),
    )
    attended, log_total = attention_forward(queries, all_keys, all_values, query_pos, segment)
    spread = to_features(to_half(attended))
    middle = input_rows + feature_sums(product_right(spread, full_out)) + b_out
    normed2, scaled2, scale2 = norm_forward(middle, ln2_gain, ln2_bias)
    hidden_pre = product(normed2, full_fc1) + b_fc1
    activated, gate_pull = jax.vjp(smooth_gate, hidden_pre)
    hidden = to_half(activated)
    output = middle + feature_sums(product_right(hidden, full_fc2)) + b_fc2
    grad_mlp = to_half(cotangent_rows)
    grad_mlp_full = feature_rows(grad_mlp)
    grad_hidden = product(grad_mlp_full, full_fc2)
    grad_pre = to_half(gate_pull(grad_hidden)[0])
    grad_fc2_t = product_left(grad_mlp_full, hidden)
    grad_fc1 = product_left(normed2, grad_pre)
    grad_normed2 = feature_sums(product_right(grad_pre, full_fc1))
    back_second, gain2_grad, shift2_grad = norm_backward(grad_normed2, scaled2, scale2, ln2_gain)
    grad_middle = cotangent_rows + back_second
    grad_branch = to_half(grad_middle)
    grad_branch_full = feature_rows(grad_branch)
    grad_out_t = product_left(grad_branch_full, spread)
    grad_spread = to_half(product(grad_branch_full, full_out))
    grad_attended = to_heads(grad_spread)
    grad_q_heads, grad_k_part, grad_v_part = attention_backward(
        queries, all_keys, all_values, query_pos, segment, log_total, grad_attended
    )
    grad_query_raw = to_features(to_half(grad_q_heads)).astype(jnp.float32) * scaling
    grad_query = to_half(grad_query_raw)
    key_total, value_total = (
        lax.psum_scatter(
            grad_k_part.astype(jnp.bfloat16), "col", scatter_dimension=1, tiled=True
        ).astype(jnp.float32),
        lax.psum_scatter(
            grad_v_part.astype(jnp.bfloat16), "col", scatter_dimension=1, tiled=True
        ).astype(jnp.float32),
    )
    grad_key = to_half(key_total)
    grad_value = to_half(value_total)
    grad_normed1 = feature_sums(
        product_right(grad_query, full_query)
        + product_right(grad_key, full_key)
        + product_right(grad_value, full_value)
    )
    back_first, gain1_grad, shift1_grad = norm_backward(grad_normed1, scaled1, scale1, ln1_gain)
    grad_input = grad_middle + back_first
    weight_sums = (
        lax.psum_scatter(
            product_left(normed1, grad_query).astype(jnp.bfloat16),
            "row",
            scatter_dimension=0,
            tiled=True,
        ).astype(jnp.float32),
        lax.psum_scatter(
            product_left(normed1, grad_key).astype(jnp.bfloat16),
            "row",
            scatter_dimension=0,
            tiled=True,
        ).astype(jnp.float32),
        lax.psum_scatter(
            product_left(normed1, grad_value).astype(jnp.bfloat16),
            "row",
            scatter_dimension=0,
            tiled=True,
        ).astype(jnp.float32),
        lax.psum_scatter(
            grad_out_t.astype(jnp.bfloat16), "row", scatter_dimension=0, tiled=True
        ).astype(jnp.float32),
        lax.psum_scatter(
            grad_fc1.astype(jnp.bfloat16), "row", scatter_dimension=0, tiled=True
        ).astype(jnp.float32),
        lax.psum_scatter(
            grad_fc2_t.astype(jnp.bfloat16), "row", scatter_dimension=0, tiled=True
        ).astype(jnp.float32),
    )
    vector_sums = lax.psum(
        (
            gain1_grad,
            shift1_grad,
            column_sum(grad_query_raw),
            column_sum(grad_value),
            column_sum(grad_branch),
            gain2_grad,
            shift2_grad,
            column_sum(grad_pre),
            column_sum(grad_mlp),
        ),
        "row",
    )
    return (
        output.T,
        grad_input.T,
        vector_sums[0],
        vector_sums[1],
        weight_sums[0],
        weight_sums[1],
        weight_sums[2],
        vector_sums[2],
        vector_sums[3],
        weight_sums[3].T,
        vector_sums[4],
        vector_sums[5],
        vector_sums[6],
        weight_sums[4],
        vector_sums[7],
        weight_sums[5].T,
        vector_sums[8],
    )


VMEM_LIMIT = 56 * 1024 * 1024
MESH_IDS = pl.DeviceIdType.MESH


def left_product(first_op, second_op, **extra):
    return lax.dot_general(
        first_op, second_op, (((0,), (0,)), ((), ())), preferred_element_type=jnp.float32, **extra
    )


def right_product(first_op, second_op, **extra):
    return lax.dot_general(
        first_op, second_op, (((1,), (1,)), ((), ())), preferred_element_type=jnp.float32, **extra
    )


def remote(source, target, send_sem, recv_sem, device):
    return pltpu.make_async_remote_copy(
        src_ref=source,
        dst_ref=target,
        send_sem=send_sem,
        recv_sem=recv_sem,
        device_id=device,
        device_id_type=MESH_IDS,
    )


class Place:
    def __init__(self):
        self.col = lax.axis_index("col")
        self.row = lax.axis_index("row")
        self.core_peer = self.col + 1 - 2 * lax.rem(self.col, 2)
        self.chip_peer = lax.rem(self.col + 2, 4)
        self.far_peer = lax.rem(self.core_peer + 2, 4)
        self.z = self.row // 2
        self.y = lax.rem(self.row, 2)
        self.y_peer = self.row + 1 - 2 * self.y


def greet(place, rows_too):
    barrier = pltpu.get_barrier_semaphore()
    count = 3
    for step in range(1, 4):
        peer = lax.rem(place.col + step, 4)
        pl.semaphore_signal(barrier, inc=1, device_id={"col": peer}, device_id_type=MESH_IDS)
    if rows_too:
        count += 7
        for step in range(1, 8):
            peer = lax.rem(place.row + step, 8)
            pl.semaphore_signal(barrier, inc=1, device_id={"row": peer}, device_id_type=MESH_IDS)
    pl.semaphore_wait(barrier, count)


class ColGather:
    def __init__(self, place, buf, send, recv):
        self.place, self.buf, self.send, self.recv = place, buf, send, recv
        self.size = buf.shape[0] // 4

    def block(self, index):
        return self.buf.at[pl.ds(pl.multiple_of(index * self.size, self.size), self.size)]

    def start(self):
        own = self.block(self.place.col)
        self.chip = remote(own, own, self.send.at[0], self.recv.at[0], {"col": self.place.chip_peer})
        self.core = remote(own, own, self.send.at[1], self.recv.at[1], {"col": self.place.core_peer})
        self.chip.start()
        self.core.start()

    def forward(self):
        self.chip.wait_recv()
        got = self.block(self.place.chip_peer)
        self.onward = remote(got, got, self.send.at[2], self.recv.at[2], {"col": self.place.core_peer})
        self.onward.start()

    def finish(self):
        self.chip.wait_send()
        self.core.wait()
        self.onward.wait()


class ColScatter:
    def __init__(self, place, part, slots, stage, send, recv):
        self.place, self.part, self.slots, self.stage = place, part, slots, stage
        self.send, self.recv = send, recv
        self.size = part.shape[0] // 4

    def block(self, index):
        return self.part.at[pl.ds(pl.multiple_of(index * self.size, self.size), self.size)]

    def start(self):
        place = self.place
        peer = {"col": place.core_peer}
        self.far = remote(
            self.block(place.far_peer), self.slots.at[0], self.send.at[0], self.recv.at[0], peer
        )
        self.near = remote(
            self.block(place.core_peer), self.slots.at[1], self.send.at[1], self.recv.at[1], peer
        )
        self.far.start()
        self.near.start()

    def forward(self):
        self.far.wait_recv()
        mixed = self.block(self.place.chip_peer)[...].astype(jnp.float32) + self.slots[0].astype(
            jnp.float32
        )
        self.stage[...] = mixed.astype(self.stage.dtype)
        self.cross = remote(
            self.stage,
            self.slots.at[2],
            self.send.at[2],
            self.recv.at[2],
            {"col": self.place.chip_peer},
        )
        self.cross.start()

    def finish(self):
        self.far.wait_send()
        self.near.wait()
        self.cross.wait()
        own = self.block(self.place.col)[...].astype(jnp.float32)
        return own + self.slots[1].astype(jnp.float32) + self.slots[2].astype(jnp.float32)


def exchange_sums(place, first, second, stat, send, recv):
    stat[place.col, 0:1, :] = first
    stat[place.col, 1:2, :] = second
    copies = []
    for step in range(1, 4):
        peer = lax.rem(place.col + step, 4)
        copy = remote(
            stat.at[place.col],
            stat.at[place.col],
            send.at[step - 1],
            recv.at[step - 1],
            {"col": peer},
        )
        copy.start()
        copies.append(copy)
    for copy in copies:
        copy.wait()
    total = stat[0] + stat[1] + stat[2] + stat[3]
    return total[0:1], total[1:2]


def norm_stats(place, values, width, stat, send, recv):
    sums, squares = exchange_sums(
        place,
        jnp.sum(values, axis=0, keepdims=True),
        jnp.sum(values * values, axis=0, keepdims=True),
        stat,
        send,
        recv,
    )
    mean = sums / width
    scale = lax.rsqrt(squares / width - mean * mean + EPS)
    return mean, scale


def norm_back(place, upstream, scaled, scale, gain, width, stat, send, recv):
    weighted = upstream * gain
    sums, along = exchange_sums(
        place,
        jnp.sum(weighted, axis=0, keepdims=True),
        jnp.sum(weighted * scaled, axis=0, keepdims=True),
        stat,
        send,
        recv,
    )
    return scale * (weighted - sums / width - scaled * (along / width))


def token_sum(values):
    ones = jnp.ones((8, values.shape[1]), jnp.float32)
    return right_product(ones, values, precision=lax.Precision.HIGHEST)[0:1]


class LineGather:
    def __init__(self, place, buf, columns, size, stride, offset, send, recv):
        self.place, self.buf, self.columns, self.size = place, buf, columns, size
        self.stride, self.offset, self.send, self.recv = stride, offset, send, recv

    def copy(self, hop, way):
        source = self.place.z - way * hop
        start = pl.multiple_of(jnp.clip(source, 0, 3) * self.stride + self.offset, 16)
        block = self.buf.at[pl.ds(start, self.size), self.columns]
        slot = 4 * (1 if way < 0 else 0)
        target = jnp.clip(self.place.row + 2 * way, 0, 7)
        return remote(
            block, block, self.send.at[slot + hop], self.recv.at[slot + hop + 1], {"row": target}
        )

    def arrived(self, hop, way):
        slot = 4 * (1 if way < 0 else 0)
        start = pl.multiple_of(
            jnp.clip(self.place.z - way * hop, 0, 3) * self.stride + self.offset, 16
        )
        block = self.buf.at[pl.ds(start, self.size), self.columns]
        pltpu.make_async_copy(block, block, self.recv.at[slot + hop]).wait()

    def has(self, hop, way):
        return self.place.z >= hop if way > 0 else self.place.z + hop <= 3

    def sends(self, hop, way):
        more = self.place.z < 3 if way > 0 else self.place.z > 0
        return jnp.logical_and(self.has(hop, way), more)

    def start(self):
        for way in (1, -1):

            @pl.when(self.sends(0, way))
            def _():
                self.copy(0, way).start()

    def step(self, hop):
        for way in (1, -1):

            @pl.when(self.has(hop, way))
            def _():
                self.arrived(hop, way)

            if hop < 3:

                @pl.when(self.sends(hop, way))
                def _():
                    self.copy(hop, way).start()

    def finish(self):
        for hop in range(3):
            for way in (1, -1):

                @pl.when(self.sends(hop, way))
                def _():
                    self.copy(hop, way).wait_send()


class LineScatter:
    def __init__(self, place, block, right, left, send, recv):
        self.place, self.block, self.right, self.left = place, block, right, left
        self.send, self.recv = send, recv

    def copy(self, target_z, way):
        slots = self.right if way > 0 else self.left
        base = 0 if way > 0 else 4
        device = {"row": jnp.clip(self.place.row + 2 * way, 0, 7)}
        return remote(
            slots.at[target_z],
            slots.at[target_z],
            self.send.at[base + target_z],
            self.recv.at[base + target_z],
            device,
        )

    def step(self, index):
        z = self.place.z
        for way, target_z in ((1, 3 - index), (-1, index)):
            slots = self.right if way > 0 else self.left
            relays = z < target_z if way > 0 else z > target_z
            edge = z == 0 if way > 0 else z == 3
            inner = z > 0 if way > 0 else z < 3

            @pl.when(jnp.logical_and(relays, edge))
            def _():
                slots[target_z] = self.block(target_z)[...]

            @pl.when(jnp.logical_and(relays, inner))
            def _():
                self.copy(target_z, way).wait_recv()
                mixed = slots[target_z].astype(jnp.float32) + self.block(target_z)[...].astype(
                    jnp.float32
                )
                slots[target_z] = mixed.astype(slots.dtype)

            @pl.when(relays)
            def _():
                self.copy(target_z, way).start()

    def finish(self, total):
        z = self.place.z
        for target_z in range(4):

            @pl.when(z == target_z)
            def _():
                total[...] = self.block(target_z)[...].astype(jnp.float32)
                if target_z > 0:
                    self.copy(target_z, 1).wait_recv()
                    total[...] += self.right[target_z].astype(jnp.float32)
                if target_z < 3:
                    self.copy(target_z, -1).wait_recv()
                    total[...] += self.left[target_z].astype(jnp.float32)

            if target_z > 0:

                @pl.when(z < target_z)
                def _():
                    self.copy(target_z, 1).wait_send()

            if target_z < 3:

                @pl.when(z > target_z)
                def _():
                    self.copy(target_z, -1).wait_send()


def enter_kernel(
    x_ref, cot_ref, gain_ref, shift_ref, w_ref,
    h_ref, gm_ref, stats_ref, full_ref,
    stat, sums_send, sums_recv, h_send, h_recv, gm_send, gm_recv,
    near_send, near_recv, far_send, far_recv, y_send, y_recv,
):
    place = Place()
    greet(place, True)
    size = x_ref.shape[0]
    rows = w_ref.shape[0]
    half = w_ref.shape[1] // 2
    first, second = pl.ds(0, half), pl.ds(half, half)
    own_row = pl.multiple_of(place.row * rows, rows)
    full_ref[pl.ds(own_row, rows), :] = w_ref[...]
    own_second = full_ref.at[pl.ds(own_row, rows), second]
    y_peer = {"row": place.y_peer}
    pair = remote(own_second, own_second, y_send.at[4], y_recv.at[4], y_peer)
    pair.start()
    line_first = LineGather(
        place, full_ref, first, rows, 2 * rows, place.y * rows, near_send, near_recv
    )
    line_first.start()
    own = pl.ds(pl.multiple_of(place.col * size, size), size)
    gm_ref[own, :] = cot_ref[...].astype(gm_ref.dtype)
    values = x_ref[...]
    mean, scale = norm_stats(place, values, 4.0 * size, stat, sums_send, sums_recv)
    stats_ref[0:1, :] = mean
    stats_ref[1:2, :] = scale
    h_ref[own, :] = ((values - mean) * scale * gain_ref[...] + shift_ref[...]).astype(h_ref.dtype)
    h_gather = ColGather(place, h_ref, h_send, h_recv)
    h_gather.start()
    gm_gather = ColGather(place, gm_ref, gm_send, gm_recv)
    gm_gather.start()
    pair.wait()
    line_second = LineGather(
        place, full_ref, second, 2 * rows, 2 * rows, 0, far_send, far_recv
    )
    line_second.start()

    def across(source, slot):
        start = pl.multiple_of(source * 2 * rows + place.y * rows, rows)
        block = full_ref.at[pl.ds(start, rows), first]
        return remote(block, block, y_send.at[slot], y_recv.at[slot], y_peer)

    across(place.z, 5).start()
    line_first.step(1)
    h_gather.forward()
    line_second.step(1)
    line_first.step(2)
    gm_gather.forward()
    line_second.step(2)
    line_first.step(3)
    for source in range(4):

        @pl.when(place.z != source)
        def _():
            across(source, source).start()

    line_second.step(3)
    h_gather.finish()
    gm_gather.finish()
    across(place.z, 5).wait()
    for source in range(4):

        @pl.when(place.z != source)
        def _():
            across(source, source).wait()

    line_first.finish()
    line_second.finish()


def middle_kernel(
    part_ref, x_ref, bias_ref, gain_ref, shift_ref,
    mid_ref, h_ref, stats_ref,
    slots, stage, stat, rs_send, rs_recv, sums_send, sums_recv, h_send, h_recv,
):
    place = Place()
    greet(place, False)
    size = x_ref.shape[0]
    scatter = ColScatter(place, part_ref, slots, stage, rs_send, rs_recv)
    scatter.start()
    scatter.forward()
    values = scatter.finish() + x_ref[...] + bias_ref[...]
    mid_ref[...] = values
    mean, scale = norm_stats(place, values, 4.0 * size, stat, sums_send, sums_recv)
    stats_ref[0:1, :] = mean
    stats_ref[1:2, :] = scale
    own = pl.ds(pl.multiple_of(place.col * size, size), size)
    h_ref[own, :] = ((values - mean) * scale * gain_ref[...] + shift_ref[...]).astype(h_ref.dtype)
    gather = ColGather(place, h_ref, h_send, h_recv)
    gather.start()
    gather.forward()
    gather.finish()


def turn_kernel(
    out_part_ref, grad_part_ref, mid_ref, cot_ref, stats_ref, gain_ref, bias_ref,
    out_ref, gx_ref, ga_ref, vec_ref,
    slots, stage, out_slots, out_stage, stat,
    rs_send, rs_recv, out_send, out_recv, sums_send, sums_recv, ga_send, ga_recv,
):
    place = Place()
    greet(place, False)
    size = mid_ref.shape[0]
    scatter = ColScatter(place, grad_part_ref, slots, stage, rs_send, rs_recv)
    scatter.start()
    out_scatter = ColScatter(place, out_part_ref, out_slots, out_stage, out_send, out_recv)
    out_scatter.start()
    scatter.forward()
    mean, scale = stats_ref[0:1, :], stats_ref[1:2, :]
    upstream = scatter.finish()
    scaled = (mid_ref[...] - mean) * scale
    back = norm_back(
        place, upstream, scaled, scale, gain_ref[...], 4.0 * size, stat, sums_send, sums_recv
    )
    gx = cot_ref[...] + back
    gx_ref[...] = gx
    own = pl.ds(pl.multiple_of(place.col * size, size), size)
    ga_ref[own, :] = gx.astype(ga_ref.dtype)
    gather = ColGather(place, ga_ref, ga_send, ga_recv)
    gather.start()
    out_scatter.forward()
    vec_ref[0:1, :] = token_sum(upstream * scaled)
    vec_ref[1:2, :] = token_sum(upstream)
    gather.forward()
    out_ref[...] = out_scatter.finish() + mid_ref[...] + bias_ref[...]
    gather.finish()


def leave_kernel(
    part_ref, x_ref, stats_ref, gain_ref, gx_ref, grads_ref, vec_ref,
    gin_ref, sums_ref, vecs_ref,
    slots, stage, stat, rs_send, rs_recv, sums_send, sums_recv,
    vec_slots, vec_send, vec_recv,
    y_slots, right_a, left_a, right_b, left_b, total_b, y_stage, y_last,
    y_send, y_recv, near_send, near_recv, far_send, far_recv,
):
    place = Place()
    greet(place, True)
    size = x_ref.shape[0]
    rows = grads_ref.shape[0] // 8
    half = grads_ref.shape[1] // 2
    first, second = pl.ds(0, half), pl.ds(half, half)
    y_peer = {"row": place.y_peer}
    scatter = ColScatter(place, part_ref, slots, stage, rs_send, rs_recv)
    scatter.start()

    def across(target_z):
        start = pl.multiple_of(target_z * 2 * rows + (1 - place.y) * rows, rows)
        return remote(
            grads_ref.at[pl.ds(start, rows), first],
            y_slots.at[target_z],
            y_send.at[target_z],
            y_recv.at[target_z],
            y_peer,
        )

    for target_z in (3, 0, 2, 1):
        across(target_z).start()
    line_b = LineScatter(
        place,
        lambda k: grads_ref.at[pl.ds(k * 2 * rows, 2 * rows), second],
        right_b, left_b, far_send, far_recv,
    )
    line_b.step(0)
    scatter.forward()
    for target_z in (3, 0, 2, 1):
        across(target_z).wait()
        start = pl.multiple_of(target_z * 2 * rows + place.y * rows, rows)
        mixed = y_slots[target_z].astype(jnp.float32) + grads_ref[
            pl.ds(start, rows), first
        ].astype(jnp.float32)
        y_slots[target_z] = mixed.astype(y_slots.dtype)
    line_b.step(1)
    line_a = LineScatter(
        place, lambda k: y_slots.at[k], right_a, left_a, near_send, near_recv
    )
    line_a.step(0)
    line_b.step(2)
    line_a.step(1)
    mean, scale = stats_ref[0:1, :], stats_ref[1:2, :]
    upstream = scatter.finish()
    scaled = (x_ref[...] - mean) * scale
    vec_slots[place.row] = vec_ref[...]
    vec_slots[place.row, 10:11, 0:size] = token_sum(upstream * scaled)
    vec_slots[place.row, 11:12, 0:size] = token_sum(upstream)
    vec_copies = []
    for step in range(1, 8):
        peer = lax.rem(place.row + step, 8)
        copy = remote(
            vec_slots.at[place.row],
            vec_slots.at[place.row],
            vec_send.at[step - 1],
            vec_recv.at[step - 1],
            {"row": peer},
        )
        copy.start()
        vec_copies.append(copy)
    back = norm_back(
        place, upstream, scaled, scale, gain_ref[...], 4.0 * size, stat, sums_send, sums_recv
    )
    gin_ref[...] = gx_ref[...] + back
    line_a.step(2)
    line_b.finish(total_b)
    theirs = pl.ds(pl.multiple_of((1 - place.y) * rows, rows), rows)
    y_stage[...] = total_b[theirs, :].astype(y_stage.dtype)
    last = remote(y_stage, y_last, y_send.at[4], y_recv.at[4], y_peer)
    last.start()
    line_a.finish(sums_ref.at[:, first])
    for copy in vec_copies:
        copy.wait()
    total = vec_slots[0]
    for index in range(1, 8):
        total = total + vec_slots[index]
    vecs_ref[...] = total
    last.wait()
    ours = pl.ds(pl.multiple_of(place.y * rows, rows), rows)
    sums_ref[:, second] = total_b[ours, :] + y_last[...].astype(jnp.float32)


def communicate(kernel, number, shapes, scratch, *operands):
    return pl.pallas_call(
        kernel,
        out_shape=[jax.ShapeDtypeStruct(*shape) for shape in shapes],
        in_specs=[pl.BlockSpec(memory_space=pltpu.VMEM)] * len(operands),
        out_specs=[pl.BlockSpec(memory_space=pltpu.VMEM)] * len(shapes),
        scratch_shapes=scratch,
        compiler_params=pltpu.CompilerParams(
            collective_id=number, has_side_effects=True, vmem_limit_bytes=VMEM_LIMIT
        ),
    )(*operands)


def sems(*counts):
    pairs = []
    for count in counts:
        pairs += [pltpu.SemaphoreType.DMA((count,)), pltpu.SemaphoreType.DMA((count,))]
    return pairs


def allowed_pairs(keys, start, width, key_seg, query_seg):
    key_pos = lax.broadcasted_iota(jnp.int32, (keys, width), 0)
    query_pos = lax.broadcasted_iota(jnp.int32, (keys, width), 1) + start
    return (key_seg == query_seg) & (key_pos <= query_pos)


def attend_kernel(q_ref, k_ref, v_ref, key_seg_ref, query_seg_ref, o_ref, log_ref):
    tokens = q_ref.shape[1]
    width = tokens // 4
    for start in range(0, tokens, width):
        keys = start + width
        mine = pl.ds(start, width)
        scores = left_product(k_ref[:, 0:keys], q_ref[:, mine])
        allowed = allowed_pairs(
            keys, start, width, key_seg_ref[0:keys, :], query_seg_ref[:, mine]
        )
        scores = jnp.where(allowed, scores, NEG)
        top = jnp.max(scores, axis=0, keepdims=True)
        expo = jnp.exp(scores - top)
        total = jnp.sum(expo, axis=0, keepdims=True)
        probs = (expo * (1.0 / total)).astype(jnp.bfloat16)
        o_ref[:, mine] = product(v_ref[:, 0:keys], probs).astype(o_ref.dtype)
        log_ref[0, :, mine] = top + jnp.log(total)


def attend_back_kernel(
    q_ref, k_ref, v_ref, go_ref, log_ref, key_seg_ref, query_seg_ref,
    gq_ref, gk_ref, gv_ref, gk_sum, gv_sum,
):
    tokens = q_ref.shape[1]
    width = tokens // 4
    gk_sum[...] = jnp.zeros_like(gk_sum)
    gv_sum[...] = jnp.zeros_like(gv_sum)
    for start in range(0, tokens, width):
        keys = start + width
        mine = pl.ds(start, width)
        queries, upstream = q_ref[:, mine], go_ref[:, mine]
        scores = left_product(k_ref[:, 0:keys], queries)
        allowed = allowed_pairs(
            keys, start, width, key_seg_ref[0:keys, :], query_seg_ref[:, mine]
        )
        probs = jnp.exp(jnp.where(allowed, scores, NEG) - log_ref[0, :, mine])
        grad_probs = left_product(v_ref[:, 0:keys], upstream)
        inner = jnp.sum(probs * grad_probs, axis=0, keepdims=True)
        grad_scores = (probs * (grad_probs - inner)).astype(jnp.bfloat16)
        grad_q = product(k_ref[:, 0:keys], grad_scores).astype(jnp.bfloat16)
        gq_ref[:, mine] = (grad_q.astype(jnp.float32) * HEAD_DIM ** (-0.5)).astype(gq_ref.dtype)
        gk_sum[:, 0:keys] += right_product(queries, grad_scores)
        gv_sum[:, 0:keys] += right_product(upstream, probs.astype(jnp.bfloat16))
    gk_ref[...] = gk_sum[...].astype(gk_ref.dtype)
    gv_ref[...] = gv_sum[...].astype(gv_ref.dtype)


def head_spec(tokens, offset):
    return pl.BlockSpec((HEAD_DIM, tokens), lambda head: (head + offset, 0))


def whole_spec(shape):
    return pl.BlockSpec(shape, lambda head: (0,) * len(shape))


def local_params():
    return pltpu.CompilerParams(vmem_limit_bytes=VMEM_LIMIT)


def attend(qkv, key_seg, query_seg):
    size, tokens = qkv.shape[0] // 3, qkv.shape[1]
    heads = size // HEAD_DIM
    log_spec = pl.BlockSpec((1, 1, tokens), lambda head: (head, 0, 0))
    return pl.pallas_call(
        attend_kernel,
        grid=(heads,),
        in_specs=[head_spec(tokens, part * heads) for part in range(3)]
        + [whole_spec((tokens, 1)), whole_spec((1, tokens))],
        out_specs=[head_spec(tokens, 0), log_spec],
        out_shape=[
            jax.ShapeDtypeStruct((size, tokens), jnp.bfloat16),
            jax.ShapeDtypeStruct((heads, 1, tokens), jnp.float32),
        ],
        compiler_params=local_params(),
    )(qkv, qkv, qkv, key_seg, query_seg)


def attend_back(qkv, grad_mixed, log_total, key_seg, query_seg):
    size, tokens = qkv.shape[0] // 3, qkv.shape[1]
    heads = size // HEAD_DIM
    log_spec = pl.BlockSpec((1, 1, tokens), lambda head: (head, 0, 0))
    return pl.pallas_call(
        attend_back_kernel,
        grid=(heads,),
        in_specs=[head_spec(tokens, part * heads) for part in range(3)]
        + [head_spec(tokens, 0), log_spec, whole_spec((tokens, 1)), whole_spec((1, tokens))],
        out_specs=[head_spec(tokens, 0)] * 3,
        out_shape=[jax.ShapeDtypeStruct((size, tokens), jnp.bfloat16)] * 3,
        scratch_shapes=[pltpu.VMEM((HEAD_DIM, tokens), jnp.float32)] * 2,
        compiler_params=local_params(),
    )(qkv, qkv, qkv, grad_mixed, log_total, key_seg, query_seg)


def fast_shards(
    layer_input,
    ln1_gain,
    ln1_bias,
    w_query,
    w_key,
    w_value,
    b_query,
    b_value,
    w_out,
    b_out,
    ln2_gain,
    ln2_bias,
    w_fc1,
    b_fc1,
    w_fc2,
    b_fc2,
    seq_lengths,
    cotangent,
):
    half, wide = jnp.bfloat16, jnp.float32
    size, tokens = layer_input.shape
    full = 4 * size
    rows, hidden_size = w_fc1.shape
    width = 4 * size + 2 * hidden_size
    scaling = HEAD_DIM ** (-0.5)
    seq_ends = jnp.cumsum(seq_lengths[0])
    places = jnp.arange(tokens, dtype=jnp.int32)
    segment = jnp.sum((places[:, None] >= seq_ends[None, :]).astype(jnp.int32), axis=1)
    key_seg, query_seg = segment[:, None], segment[None, :]
    packed = jnp.concatenate([w_query, w_key, w_value, w_out.T, w_fc1, w_fc2.T], axis=1)
    stat = pltpu.VMEM((4, 8, tokens), wide)
    slots = pltpu.VMEM((3, size, tokens), half)
    stage = pltpu.VMEM((size, tokens), half)

    normed1, grad_mlp, stats1, weights = communicate(
        enter_kernel,
        1,
        [((full, tokens), half), ((full, tokens), half), ((8, tokens), wide), ((8 * rows, width), half)],
        [stat] + sems(3, 3, 3, 8, 8, 6),
        layer_input,
        cotangent,
        ln1_gain[:, None],
        ln1_bias[:, None],
        packed,
    )
    w_qkv, w_up = weights[:, : 3 * size], weights[:, 3 * size : 4 * size]
    w_first = weights[:, 4 * size : 4 * size + hidden_size]
    w_second = weights[:, 4 * size + hidden_size :]
    qkv_bias = jnp.concatenate([b_query, jnp.zeros_like(b_query), b_value])[:, None]
    qkv_scale = jnp.where(jnp.arange(3 * size) < size, scaling, 1.0)[:, None]
    qkv = to_half((left_product(w_qkv, normed1) + qkv_bias) * qkv_scale)
    mixed, log_total = attend(qkv, key_seg, query_seg)
    middle, normed2, stats2 = communicate(
        middle_kernel,
        2,
        [((size, tokens), wide), ((full, tokens), half), ((8, tokens), wide)],
        [slots, stage, stat] + sems(3, 3, 3),
        to_half(product(w_up, mixed)),
        layer_input,
        b_out[:, None],
        ln2_gain[:, None],
        ln2_bias[:, None],
    )
    hidden_pre = left_product(w_first, normed2) + b_fc1[:, None]
    activated, gate_pull = jax.vjp(smooth_gate, hidden_pre)
    hidden = to_half(activated)
    grad_pre = to_half(gate_pull(left_product(w_second, grad_mlp))[0])
    output, grad_middle, grad_branch, norm2_sums = communicate(
        turn_kernel,
        3,
        [((size, tokens), wide), ((size, tokens), wide), ((full, tokens), half), ((8, size), wide)],
        [slots, stage, slots, stage, stat] + sems(3, 3, 3, 3),
        to_half(product(w_second, hidden)),
        to_half(product(w_first, grad_pre)),
        middle,
        cotangent,
        stats2,
        ln2_gain[:, None],
        b_fc2[:, None],
    )
    grad_mixed = to_half(left_product(w_up, grad_branch))
    grad_q, grad_k, grad_v = attend_back(qkv, grad_mixed, log_total, key_seg, query_seg)
    grad_qkv = jnp.concatenate([grad_q, grad_k, grad_v], axis=0)
    grads = jnp.concatenate(
        [
            to_half(right_product(normed1, grad_qkv)),
            to_half(right_product(grad_branch, mixed)),
            to_half(right_product(normed2, grad_pre)),
            to_half(right_product(grad_mlp, hidden)),
        ],
        axis=1,
    )

    def along(values):
        return jnp.sum(values.astype(wide), axis=1)

    vectors = jnp.concatenate(
        [
            along(grad_q)[None],
            along(grad_v)[None],
            along(to_half(grad_middle))[None],
            norm2_sums[0:2],
            along(to_half(cotangent))[None],
            along(grad_pre).reshape(hidden_size // size, size),
            jnp.zeros((6, size), wide),
        ],
        axis=0,
    )
    vectors = jnp.pad(vectors, ((0, 0), (0, 256 - size)))
    line_half = width // 2
    grad_input, sums, vector_sums = communicate(
        leave_kernel,
        4,
        [((size, tokens), wide), ((rows, width), wide), (vectors.shape, wide)],
        [slots, stage, stat]
        + sems(3, 3)
        + [pltpu.VMEM((8,) + vectors.shape, wide)]
        + sems(7)
        + [pltpu.VMEM((4, rows, line_half), half)] * 3
        + [pltpu.VMEM((4, 2 * rows, line_half), half)] * 2
        + [
            pltpu.VMEM((2 * rows, line_half), wide),
            pltpu.VMEM((rows, line_half), half),
            pltpu.VMEM((rows, line_half), half),
        ]
        + sems(5, 8, 8),
        to_half(product(w_qkv, grad_qkv)),
        layer_input,
        stats1,
        ln1_gain[:, None],
        grad_middle,
        grads,
        vectors,
    )
    vector_sums = vector_sums[:, :size]
    return (
        output,
        grad_input,
        vector_sums[10],
        vector_sums[11],
        sums[:, :size],
        sums[:, size : 2 * size],
        sums[:, 2 * size : 3 * size],
        vector_sums[0],
        vector_sums[1],
        sums[:, 3 * size : 4 * size].T,
        vector_sums[2],
        vector_sums[3],
        vector_sums[4],
        sums[:, 4 * size : 4 * size + hidden_size],
        vector_sums[6:10].reshape(-1),
        sums[:, 4 * size + hidden_size :].T,
        vector_sums[5],
    )


def solution(mesh):
    in_specs = (
        P("col", "row"),
        P("col"),
        P("col"),
        P("row", "col"),
        P("row", "col"),
        P("row", "col"),
        P("col"),
        P("col"),
        P("col", "row"),
        P("col"),
        P("col"),
        P("col"),
        P("row", "col"),
        P("col"),
        P("col", "row"),
        P("col"),
        P("row", None),
        P("col", "row"),
    )
    out_specs = (
        P("col", "row"),
        P("col", "row"),
        P("col"),
        P("col"),
        P("row", "col"),
        P("row", "col"),
        P("row", "col"),
        P("col"),
        P("col"),
        P("col", "row"),
        P("col"),
        P("col"),
        P("col"),
        P("row", "col"),
        P("col"),
        P("col", "row"),
        P("col"),
    )
    fits = mesh.shape["col"] == 4 and mesh.shape["row"] == 8
    body = fast_shards if fits else shards
    return jax.shard_map(body, mesh=mesh, in_specs=in_specs, out_specs=out_specs, check_vma=False)
```

```python
import functools

import jax
import jax.numpy as jnp
from jax import lax
from jax.experimental import pallas as pl
from jax.experimental.pallas import tpu as pltpu
from jax.sharding import PartitionSpec as P

HEADS = 12
HEAD_DIM = 64


EPS = 1e-05
NEG = -1e30


def to_half(values):
    return values.astype(jnp.bfloat16)


def product(first_op, second_op):
    return jnp.dot(first_op, second_op, preferred_element_type=jnp.float32)


def product_left(first_op, second_op):
    return lax.dot_general(
        first_op, second_op, (((0,), (0,)), ((), ())), preferred_element_type=jnp.float32
    )


def product_right(first_op, second_op):
    return lax.dot_general(
        first_op, second_op, (((1,), (1,)), ((), ())), preferred_element_type=jnp.float32
    )


def column_sum(values):
    return jnp.sum(values.astype(jnp.float32), axis=0)


def smooth_gate(values):
    return jax.nn.gelu(values, approximate=True)


def query_positions(pack_rows):
    col_count = lax.axis_size("col")
    col_index = lax.axis_index("col")
    share_rows = pack_rows // col_count
    return col_index * share_rows + jnp.arange(share_rows, dtype=jnp.int32)


def feature_rows(block_rows):
    return lax.all_gather(block_rows, "col", axis=1, tiled=True)


def feature_sums(partial_value):
    return lax.psum_scatter(partial_value, "col", scatter_dimension=1, tiled=True)


def to_heads(block_rows):
    return lax.all_to_all(block_rows, "col", split_axis=0, concat_axis=1, tiled=True)


def to_features(block_rows):
    spread = lax.all_to_all(block_rows, "col", split_axis=1, concat_axis=0, tiled=True)
    return spread


def norm_forward(block_rows, norm_gain, norm_shift):
    local_width = block_rows.shape[1]
    full_width = local_width * lax.axis_size("col")
    row_sums, row_squares = lax.psum(
        (jnp.sum(block_rows, axis=1), jnp.sum(block_rows * block_rows, axis=1)), "col"
    )
    row_mean = (row_sums / full_width)[:, None]
    variance = (row_squares / full_width)[:, None] - row_mean * row_mean
    row_scale = lax.rsqrt(variance + EPS)
    scaled = (block_rows - row_mean) * row_scale
    normed = feature_rows(to_half(scaled * norm_gain + norm_shift))
    return (normed, scaled, row_scale)


def norm_backward(upstream, scaled, row_scale, norm_gain):
    full_width = upstream.shape[1] * lax.axis_size("col")
    weighted = upstream * norm_gain
    row_sums, row_along = lax.psum(
        (jnp.sum(weighted, axis=1), jnp.sum(weighted * scaled, axis=1)), "col"
    )
    grad_rows = row_scale * (
        weighted - (row_sums / full_width)[:, None] - scaled * (row_along / full_width)[:, None]
    )
    return (grad_rows, jnp.sum(upstream * scaled, axis=0), jnp.sum(upstream, axis=0))


def split_heads(block_rows):
    return block_rows.reshape(block_rows.shape[0], HEADS, HEAD_DIM)


def masked_scores(queries, all_keys, query_pos, segment):
    scores = jnp.einsum(
        "qhd,khd->hqk",
        split_heads(queries),
        split_heads(all_keys),
        preferred_element_type=jnp.float32,
    )
    key_pos = jnp.arange(all_keys.shape[0], dtype=jnp.int32)
    allowed = (segment[query_pos][:, None] == segment[None, :]) & (
        key_pos[None, :] <= query_pos[:, None]
    )
    return jnp.where(allowed[None], scores, NEG)


def attention_forward(queries, all_keys, all_values, query_pos, segment):
    scores = masked_scores(queries, all_keys, query_pos, segment)
    row_top = jnp.max(scores, axis=2, keepdims=True)
    expo_vals = jnp.exp(scores - row_top)
    row_total = jnp.sum(expo_vals, axis=2, keepdims=True)
    attn_probs = to_half(expo_vals / row_total)
    mixed = jnp.einsum(
        "hqk,khd->qhd", attn_probs, split_heads(all_values), preferred_element_type=jnp.float32
    )
    return (mixed.reshape(queries.shape[0], -1), row_top + jnp.log(row_total))


def attention_backward(queries, all_keys, all_values, query_pos, segment, log_total, grad_mixed):
    scores = masked_scores(queries, all_keys, query_pos, segment)
    attn_probs = jnp.exp(scores - log_total)
    grad_heads = split_heads(grad_mixed)
    grad_probs = jnp.einsum(
        "qhd,khd->hqk", grad_heads, split_heads(all_values), preferred_element_type=jnp.float32
    )
    row_inner = jnp.sum(attn_probs * grad_probs, axis=2, keepdims=True)
    grad_scores = to_half(attn_probs * (grad_probs - row_inner))
    grad_queries = jnp.einsum(
        "hqk,khd->qhd", grad_scores, split_heads(all_keys), preferred_element_type=jnp.float32
    )
    grad_keys = jnp.einsum(
        "hqk,qhd->khd", grad_scores, split_heads(queries), preferred_element_type=jnp.float32
    )
    grad_values = jnp.einsum(
        "hqk,qhd->khd", to_half(attn_probs), grad_heads, preferred_element_type=jnp.float32
    )
    key_count = all_keys.shape[0]
    return (
        grad_queries.reshape(queries.shape[0], -1),
        grad_keys.reshape(key_count, -1),
        grad_values.reshape(key_count, -1),
    )


def shards(
    layer_input,
    ln1_gain,
    ln1_bias,
    w_query,
    w_key,
    w_value,
    b_query,
    b_value,
    w_out,
    b_out,
    ln2_gain,
    ln2_bias,
    w_fc1,
    b_fc1,
    w_fc2,
    b_fc2,
    seq_lengths,
    cotangent,
):
    scaling = HEAD_DIM ** (-0.5)
    input_rows = layer_input.T
    cotangent_rows = cotangent.T
    pack_rows = input_rows.shape[0]
    seq_ends = jnp.cumsum(seq_lengths[0])
    places = jnp.arange(pack_rows, dtype=jnp.int32)
    segment = jnp.sum((places[:, None] >= seq_ends[None, :]).astype(jnp.int32), axis=1)
    query_pos = query_positions(pack_rows)
    gathered = (
        lax.all_gather(w_query, "row", axis=0, tiled=True),
        lax.all_gather(w_key, "row", axis=0, tiled=True),
        lax.all_gather(w_value, "row", axis=0, tiled=True),
        lax.all_gather(w_fc1, "row", axis=0, tiled=True),
        lax.all_gather(w_out.T, "row", axis=0, tiled=True),
        lax.all_gather(w_fc2.T, "row", axis=0, tiled=True),
    )
    full_query, full_key, full_value, full_fc1, full_out, full_fc2 = gathered
    normed1, scaled1, scale1 = norm_forward(input_rows, ln1_gain, ln1_bias)
    query_part = to_half((product(normed1, full_query) + b_query) * scaling)
    key_part = to_half(product(normed1, full_key))
    value_part = to_half(product(normed1, full_value) + b_value)
    queries = to_heads(query_part)
    all_keys, all_values = (
        lax.all_gather(key_part, "col", axis=1, tiled=True),
        lax.all_gather(value_part, "col", axis=1, tiled=True),
    )
    attended, log_total = attention_forward(queries, all_keys, all_values, query_pos, segment)
    spread = to_features(to_half(attended))
    middle = input_rows + feature_sums(product_right(spread, full_out)) + b_out
    normed2, scaled2, scale2 = norm_forward(middle, ln2_gain, ln2_bias)
    hidden_pre = product(normed2, full_fc1) + b_fc1
    activated, gate_pull = jax.vjp(smooth_gate, hidden_pre)
    hidden = to_half(activated)
    output = middle + feature_sums(product_right(hidden, full_fc2)) + b_fc2
    grad_mlp = to_half(cotangent_rows)
    grad_mlp_full = feature_rows(grad_mlp)
    grad_hidden = product(grad_mlp_full, full_fc2)
    grad_pre = to_half(gate_pull(grad_hidden)[0])
    grad_fc2_t = product_left(grad_mlp_full, hidden)
    grad_fc1 = product_left(normed2, grad_pre)
    grad_normed2 = feature_sums(product_right(grad_pre, full_fc1))
    back_second, gain2_grad, shift2_grad = norm_backward(grad_normed2, scaled2, scale2, ln2_gain)
    grad_middle = cotangent_rows + back_second
    grad_branch = to_half(grad_middle)
    grad_branch_full = feature_rows(grad_branch)
    grad_out_t = product_left(grad_branch_full, spread)
    grad_spread = to_half(product(grad_branch_full, full_out))
    grad_attended = to_heads(grad_spread)
    grad_q_heads, grad_k_part, grad_v_part = attention_backward(
        queries, all_keys, all_values, query_pos, segment, log_total, grad_attended
    )
    grad_query_raw = to_features(to_half(grad_q_heads)).astype(jnp.float32) * scaling
    grad_query = to_half(grad_query_raw)
    key_total, value_total = (
        lax.psum_scatter(
            grad_k_part.astype(jnp.bfloat16), "col", scatter_dimension=1, tiled=True
        ).astype(jnp.float32),
        lax.psum_scatter(
            grad_v_part.astype(jnp.bfloat16), "col", scatter_dimension=1, tiled=True
        ).astype(jnp.float32),
    )
    grad_key = to_half(key_total)
    grad_value = to_half(value_total)
    grad_normed1 = feature_sums(
        product_right(grad_query, full_query)
        + product_right(grad_key, full_key)
        + product_right(grad_value, full_value)
    )
    back_first, gain1_grad, shift1_grad = norm_backward(grad_normed1, scaled1, scale1, ln1_gain)
    grad_input = grad_middle + back_first
    weight_sums = (
        lax.psum_scatter(
            product_left(normed1, grad_query).astype(jnp.bfloat16),
            "row",
            scatter_dimension=0,
            tiled=True,
        ).astype(jnp.float32),
        lax.psum_scatter(
            product_left(normed1, grad_key).astype(jnp.bfloat16),
            "row",
            scatter_dimension=0,
            tiled=True,
        ).astype(jnp.float32),
        lax.psum_scatter(
            product_left(normed1, grad_value).astype(jnp.bfloat16),
            "row",
            scatter_dimension=0,
            tiled=True,
        ).astype(jnp.float32),
        lax.psum_scatter(
            grad_out_t.astype(jnp.bfloat16), "row", scatter_dimension=0, tiled=True
        ).astype(jnp.float32),
        lax.psum_scatter(
            grad_fc1.astype(jnp.bfloat16), "row", scatter_dimension=0, tiled=True
        ).astype(jnp.float32),
        lax.psum_scatter(
            grad_fc2_t.astype(jnp.bfloat16), "row", scatter_dimension=0, tiled=True
        ).astype(jnp.float32),
    )
    vector_sums = lax.psum(
        (
            gain1_grad,
            shift1_grad,
            column_sum(grad_query_raw),
            column_sum(grad_value),
            column_sum(grad_branch),
            gain2_grad,
            shift2_grad,
            column_sum(grad_pre),
            column_sum(grad_mlp),
        ),
        "row",
    )
    return (
        output.T,
        grad_input.T,
        vector_sums[0],
        vector_sums[1],
        weight_sums[0],
        weight_sums[1],
        weight_sums[2],
        vector_sums[2],
        vector_sums[3],
        weight_sums[3].T,
        vector_sums[4],
        vector_sums[5],
        vector_sums[6],
        weight_sums[4],
        vector_sums[7],
        weight_sums[5].T,
        vector_sums[8],
    )


VMEM_LIMIT = 56 * 1024 * 1024
MESH_IDS = pl.DeviceIdType.MESH


def left_product(first_op, second_op, **extra):
    return lax.dot_general(
        first_op, second_op, (((0,), (0,)), ((), ())), preferred_element_type=jnp.float32, **extra
    )


def right_product(first_op, second_op, **extra):
    return lax.dot_general(
        first_op, second_op, (((1,), (1,)), ((), ())), preferred_element_type=jnp.float32, **extra
    )


def remote(source, target, send_sem, recv_sem, device):
    return pltpu.make_async_remote_copy(
        src_ref=source,
        dst_ref=target,
        send_sem=send_sem,
        recv_sem=recv_sem,
        device_id=device,
        device_id_type=MESH_IDS,
    )


class Place:
    def __init__(self):
        self.col = lax.axis_index("col")
        self.row = lax.axis_index("row")
        self.core_peer = self.col + 1 - 2 * lax.rem(self.col, 2)
        self.chip_peer = lax.rem(self.col + 2, 4)
        self.far_peer = lax.rem(self.core_peer + 2, 4)
        self.z = self.row // 2
        self.y = lax.rem(self.row, 2)
        self.y_peer = self.row + 1 - 2 * self.y


def greet(place, rows_too):
    barrier = pltpu.get_barrier_semaphore()
    count = 3
    for step in range(1, 4):
        peer = lax.rem(place.col + step, 4)
        pl.semaphore_signal(barrier, inc=1, device_id={"col": peer}, device_id_type=MESH_IDS)
    if rows_too:
        count += 7
        for step in range(1, 8):
            peer = lax.rem(place.row + step, 8)
            pl.semaphore_signal(barrier, inc=1, device_id={"row": peer}, device_id_type=MESH_IDS)
    pl.semaphore_wait(barrier, count)


class ColGather:
    def __init__(self, place, buf, columns, send, recv, base):
        self.place, self.buf, self.columns = place, buf, columns
        self.send, self.recv, self.base = send, recv, base
        self.size = buf.shape[0] // 4

    def block(self, index):
        rows = pl.ds(pl.multiple_of(index * self.size, self.size), self.size)
        return self.buf.at[rows, self.columns]

    def move(self, slot, source, device):
        slot += self.base
        return remote(source, source, self.send.at[slot], self.recv.at[slot], {"col": device})

    def start(self):
        own = self.block(self.place.col)
        self.chip = self.move(0, own, self.place.chip_peer)
        self.core = self.move(1, own, self.place.core_peer)
        self.chip.start()
        self.core.start()

    def forward(self):
        self.chip.wait_recv()
        got = self.block(self.place.chip_peer)
        self.onward = self.move(2, got, self.place.core_peer)
        self.onward.start()

    def finish(self):
        self.chip.wait_send()
        self.core.wait()
        self.onward.wait()


class ColScatter:
    def __init__(self, place, part, slots, stage, columns, send, recv, base):
        self.place, self.part, self.columns = place, part, columns
        self.slots, self.stage = slots, stage
        self.send, self.recv, self.base = send, recv, base
        self.size = part.shape[0] // 4

    def block(self, index):
        rows = pl.ds(pl.multiple_of(index * self.size, self.size), self.size)
        return self.part.at[rows, self.columns]

    def slot(self, index):
        return self.slots.at[index, :, self.columns]

    def move(self, slot, source, device):
        sem = slot + self.base
        return remote(
            source, self.slot(slot), self.send.at[sem], self.recv.at[sem], {"col": device}
        )

    def start(self):
        place = self.place
        self.far = self.move(0, self.block(place.far_peer), place.core_peer)
        self.far.start()
        self.near = self.move(1, self.block(place.core_peer), place.core_peer)
        self.near.start()

    def forward(self):
        self.far.wait_recv()
        mixed = self.block(self.place.chip_peer)[...].astype(jnp.float32) + self.slot(0)[
            ...
        ].astype(jnp.float32)
        staged = self.stage.at[:, self.columns]
        staged[...] = mixed.astype(self.stage.dtype)
        self.cross = self.move(2, staged, self.place.chip_peer)
        self.cross.start()

    def finish(self):
        self.far.wait_send()
        self.near.wait()
        self.cross.wait()
        own = self.block(self.place.col)[...].astype(jnp.float32)
        return own + self.slot(1)[...].astype(jnp.float32) + self.slot(2)[...].astype(jnp.float32)


class ColSums:
    def __init__(self, place, first, second, stat, columns, send, recv, base):
        self.stat, self.columns = stat, columns
        stat[place.col, 0:1, columns] = first
        stat[place.col, 1:2, columns] = second
        own = stat.at[place.col, :, columns]
        self.copies = []
        for step in range(1, 4):
            peer = lax.rem(place.col + step, 4)
            sem = base + step - 1
            copy = remote(own, own, send.at[sem], recv.at[sem], {"col": peer})
            copy.start()
            self.copies.append(copy)

    def finish(self):
        for copy in self.copies:
            copy.wait()
        part = [self.stat[index, :, self.columns] for index in range(4)]
        total = part[0] + part[1] + part[2] + part[3]
        return total[0:1], total[1:2]


def begin_stats(place, values, *rest):
    return ColSums(
        place,
        jnp.sum(values, axis=0, keepdims=True),
        jnp.sum(values * values, axis=0, keepdims=True),
        *rest,
    )


def end_stats(sums, width):
    total, squares = sums.finish()
    mean = total / width
    return mean, lax.rsqrt(squares / width - mean * mean + EPS)


def begin_back(place, upstream, scaled, gain, *rest):
    weighted = upstream * gain
    return ColSums(
        place,
        jnp.sum(weighted, axis=0, keepdims=True),
        jnp.sum(weighted * scaled, axis=0, keepdims=True),
        *rest,
    )


def end_back(sums, upstream, scaled, scale, gain, width):
    total, along = sums.finish()
    return scale * (upstream * gain - total / width - scaled * (along / width))


def token_sum(values):
    ones = jnp.ones((8, values.shape[1]), jnp.float32)
    return right_product(ones, values, precision=lax.Precision.HIGHEST)[0:1]


class LineGather:
    def __init__(self, place, buf, columns, size, stride, offset, send, recv, onward=None):
        self.place, self.buf, self.columns, self.size = place, buf, columns, size
        self.stride, self.offset, self.send, self.recv = stride, offset, send, recv
        self.onward = onward

    def copy(self, hop, way):
        source = self.place.z - way * hop
        start = pl.multiple_of(jnp.clip(source, 0, 3) * self.stride + self.offset, 16)
        block = self.buf.at[pl.ds(start, self.size), self.columns]
        slot = 4 * (1 if way < 0 else 0)
        target = jnp.clip(self.place.row + 2 * way, 0, 7)
        return remote(
            block, block, self.send.at[slot + hop], self.recv.at[slot + hop + 1], {"row": target}
        )

    def arrived(self, hop, way):
        slot = 4 * (1 if way < 0 else 0)
        start = pl.multiple_of(
            jnp.clip(self.place.z - way * hop, 0, 3) * self.stride + self.offset, 16
        )
        block = self.buf.at[pl.ds(start, self.size), self.columns]
        pltpu.make_async_copy(block, block, self.recv.at[slot + hop]).wait()

    def has(self, hop, way):
        return self.place.z >= hop if way > 0 else self.place.z + hop <= 3

    def sends(self, hop, way):
        more = self.place.z < 3 if way > 0 else self.place.z > 0
        return jnp.logical_and(self.has(hop, way), more)

    def start(self):
        for way in (1, -1):

            @pl.when(self.sends(0, way))
            def _():
                self.copy(0, way).start()

    def step(self, hop):
        for way in (1, -1):

            @pl.when(self.has(hop, way))
            def _():
                self.arrived(hop, way)
                if self.onward is not None:
                    self.onward(hop, way).start()

            if hop < 3:

                @pl.when(self.sends(hop, way))
                def _():
                    self.copy(hop, way).start()

    def finish(self):
        if self.onward is not None:
            for hop in range(1, 4):
                for way in (1, -1):

                    @pl.when(self.has(hop, way))
                    def _():
                        self.onward(hop, way).wait()

        for hop in range(3):
            for way in (1, -1):

                @pl.when(self.sends(hop, way))
                def _():
                    self.copy(hop, way).wait_send()


class LineScatter:
    def __init__(self, place, block, right, left, send, recv):
        self.place, self.block, self.right, self.left = place, block, right, left
        self.send, self.recv = send, recv

    def copy(self, target_z, way):
        slots = self.right if way > 0 else self.left
        base = 0 if way > 0 else 4
        device = {"row": jnp.clip(self.place.row + 2 * way, 0, 7)}
        return remote(
            slots.at[target_z],
            slots.at[target_z],
            self.send.at[base + target_z],
            self.recv.at[base + target_z],
            device,
        )

    def step(self, index):
        z = self.place.z
        for way, target_z in ((1, 3 - index), (-1, index)):
            slots = self.right if way > 0 else self.left
            relays = z < target_z if way > 0 else z > target_z
            edge = z == 0 if way > 0 else z == 3
            inner = z > 0 if way > 0 else z < 3

            @pl.when(jnp.logical_and(relays, edge))
            def _():
                slots[target_z] = self.block(target_z)[...]

            @pl.when(jnp.logical_and(relays, inner))
            def _():
                self.copy(target_z, way).wait_recv()
                mixed = slots[target_z].astype(jnp.float32) + self.block(target_z)[...].astype(
                    jnp.float32
                )
                slots[target_z] = mixed.astype(slots.dtype)

            @pl.when(relays)
            def _():
                self.copy(target_z, way).start()

    def finish(self, total):
        z = self.place.z
        for target_z in range(4):

            @pl.when(z == target_z)
            def _():
                total[...] = self.block(target_z)[...].astype(jnp.float32)
                if target_z > 0:
                    self.copy(target_z, 1).wait_recv()
                    total[...] += self.right[target_z].astype(jnp.float32)
                if target_z < 3:
                    self.copy(target_z, -1).wait_recv()
                    total[...] += self.left[target_z].astype(jnp.float32)

            if target_z > 0:

                @pl.when(z < target_z)
                def _():
                    self.copy(target_z, 1).wait_send()

            if target_z < 3:

                @pl.when(z > target_z)
                def _():
                    self.copy(target_z, -1).wait_send()


def row_gather_scratch():
    return sems(8, 8, 8)


class RowGather:
    def __init__(self, place, first, second, rows, send_a, recv_a, send_b, recv_b, y_send, y_recv):
        self.place, self.rows = place, rows
        self.first, self.first_columns = first
        self.second, self.second_columns = second
        self.y_send, self.y_recv = y_send, y_recv
        self.line_a = LineGather(
            place, self.first, self.first_columns, rows, 2 * rows, place.y * rows,
            send_a, recv_a, self.onward,
        )
        self.line_b = LineGather(
            place, self.second, self.second_columns, 2 * rows, 2 * rows, 0, send_b, recv_b
        )

    def across(self, buf, columns, source_z, slot):
        start = pl.multiple_of(source_z * 2 * self.rows + self.place.y * self.rows, self.rows)
        block = buf.at[pl.ds(start, self.rows), columns]
        peer = {"row": self.place.y_peer}
        return remote(block, block, self.y_send.at[slot], self.y_recv.at[slot], peer)

    def onward(self, hop, way):
        source = jnp.clip(self.place.z - way * hop, 0, 3)
        slot = hop if way > 0 else hop + 3
        return self.across(self.first, self.first_columns, source, slot)

    def start(self):
        self.pair = self.across(self.second, self.second_columns, self.place.z, 7)
        self.pair.start()
        self.line_a.start()

    def second_start(self):
        self.pair.wait()
        self.line_b.start()
        self.mine = self.onward(0, 1)
        self.mine.start()

    def step(self, hop):
        self.line_a.step(hop)
        self.line_b.step(hop)

    def finish(self):
        self.mine.wait()
        self.line_a.finish()
        self.line_b.finish()


def row_scatter_scratch(rows, columns, half, wide):
    return (
        [pltpu.VMEM((4, rows, columns), half)] * 3
        + [pltpu.VMEM((4, 2 * rows, columns), half)] * 2
        + [
            pltpu.VMEM((2 * rows, columns), wide),
            pltpu.VMEM((rows, columns), half),
            pltpu.VMEM((rows, columns), half),
        ]
        + sems(5, 8, 8)
    )


class RowScatter:
    def __init__(
        self, place, first, second, rows, slots, right_a, left_a, right_b, left_b,
        total, stage, last, y_send, y_recv, send_a, recv_a, send_b, recv_b,
    ):
        self.place, self.rows, self.slots = place, rows, slots
        self.first, self.first_columns = first
        self.second, self.second_columns = second
        self.total, self.stage, self.last = total, stage, last
        self.y_send, self.y_recv = y_send, y_recv
        self.line_a = LineScatter(place, lambda k: slots.at[k], right_a, left_a, send_a, recv_a)
        self.line_b = LineScatter(
            place,
            lambda k: self.second.at[pl.ds(k * 2 * rows, 2 * rows), self.second_columns],
            right_b, left_b, send_b, recv_b,
        )

    def block(self, target_z, target_y):
        start = pl.multiple_of(target_z * 2 * self.rows + target_y * self.rows, self.rows)
        return self.first.at[pl.ds(start, self.rows), self.first_columns]

    def start(self):
        self.copies = {}
        for target_z in (3, 0, 2, 1):
            self.copies[target_z] = remote(
                self.block(target_z, 1 - self.place.y),
                self.slots.at[target_z],
                self.y_send.at[target_z],
                self.y_recv.at[target_z],
                {"row": self.place.y_peer},
            )
            self.copies[target_z].start()
        self.line_b.step(0)

    def mix(self, target_z):
        self.copies[target_z].wait()
        mixed = self.slots[target_z].astype(jnp.float32) + self.block(target_z, self.place.y)[
            ...
        ].astype(jnp.float32)
        self.slots[target_z] = mixed.astype(self.slots.dtype)

    def second_start(self):
        self.mix(3)
        self.mix(0)
        self.line_a.step(0)
        self.mix(2)
        self.mix(1)

    def third(self):
        self.line_b.step(1)
        self.line_a.step(1)

    def fourth(self):
        self.line_b.step(2)
        self.line_a.step(2)

    def fifth(self):
        rows = self.rows
        self.line_b.finish(self.total)
        theirs = pl.ds(pl.multiple_of((1 - self.place.y) * rows, rows), rows)
        self.stage[...] = self.total[theirs, :].astype(self.stage.dtype)
        self.final = remote(
            self.stage, self.last, self.y_send.at[4], self.y_recv.at[4], {"row": self.place.y_peer}
        )
        self.final.start()

    def finish(self, first_out, second_out):
        rows = self.rows
        self.line_a.finish(first_out)
        self.final.wait()
        ours = pl.ds(pl.multiple_of(self.place.y * rows, rows), rows)
        second_out[...] = self.total[ours, :] + self.last[...].astype(jnp.float32)


CHUNKS = 2


def chunks_of(tokens):
    width = tokens // CHUNKS
    return [pl.ds(index * width, width) for index in range(CHUNKS)]


GAIN1, SHIFT1, BIAS_OUT, GAIN2, SHIFT2, BIAS_FC2 = range(6)


def enter_kernel(
    x_ref, cot_ref, par_ref, w_ref,
    h_ref, gm_ref, stats_ref, full_ref,
    stat, sums_send, sums_recv, h_send, h_recv, gm_send, gm_recv, *row_scratch,
):
    place = Place()
    greet(place, True)
    size = x_ref.shape[0]
    rows = w_ref.shape[0]
    half = w_ref.shape[1] // 2
    chunks = chunks_of(x_ref.shape[1])
    own = pl.ds(pl.multiple_of(place.col * size, size), size)
    full_ref[pl.ds(pl.multiple_of(place.row * rows, rows), rows), :] = w_ref[...]
    gather = RowGather(
        place, (full_ref, pl.ds(0, half)), (full_ref, pl.ds(half, half)), rows, *row_scratch
    )
    gather.start()
    sums = [
        begin_stats(place, x_ref[:, cols], stat, cols, sums_send, sums_recv, 3 * index)
        for index, cols in enumerate(chunks)
    ]
    gm_ref[own, :] = cot_ref[...].astype(gm_ref.dtype)
    gathers = []
    for index, cols in enumerate(chunks):
        mean, scale = end_stats(sums[index], 4.0 * size)
        stats_ref[0:1, cols] = mean
        stats_ref[1:2, cols] = scale
        normed = (x_ref[:, cols] - mean) * scale * par_ref[:, GAIN1 : GAIN1 + 1]
        h_ref[own, cols] = (normed + par_ref[:, SHIFT1 : SHIFT1 + 1]).astype(h_ref.dtype)
        gathers.append(ColGather(place, h_ref, cols, h_send, h_recv, 3 * index))
        gathers[-1].start()
    for index, cols in enumerate(chunks):
        gathers.append(ColGather(place, gm_ref, cols, gm_send, gm_recv, 3 * index))
        gathers[-1].start()
    gather.second_start()
    gather.step(1)
    gathers[0].forward()
    gather.step(2)
    gathers[1].forward()
    gather.step(3)
    for item in gathers[2:]:
        item.forward()
    for item in gathers:
        item.finish()
    gather.finish()


def middle_kernel(
    part_ref, x_ref, par_ref, first_ref, second_ref,
    mid_ref, h_ref, stats_ref, full_first, full_second,
    slots, stage, stat, rs_send, rs_recv, sums_send, sums_recv, h_send, h_recv, *row_scratch,
):
    place = Place()
    greet(place, True)
    size = x_ref.shape[0]
    rows, columns = first_ref.shape
    chunks = chunks_of(x_ref.shape[1])
    own = pl.ds(pl.multiple_of(place.col * size, size), size)
    scatters = [
        ColScatter(place, part_ref, slots, stage, cols, rs_send, rs_recv, 3 * index)
        for index, cols in enumerate(chunks)
    ]
    for item in scatters:
        item.start()
    own_rows = pl.ds(pl.multiple_of(place.row * rows, rows), rows)
    full_first[own_rows, :] = first_ref[...]
    full_second[own_rows, :] = second_ref[...]
    everything = pl.ds(0, columns)
    gather = RowGather(
        place, (full_first, everything), (full_second, everything), rows, *row_scratch
    )
    gather.start()
    for item in scatters:
        item.forward()
    gather.second_start()
    sums, gathers = [], []

    def begin(index):
        cols = chunks[index]
        values = scatters[index].finish() + x_ref[:, cols] + par_ref[:, BIAS_OUT : BIAS_OUT + 1]
        mid_ref[:, cols] = values
        sums.append(begin_stats(place, values, stat, cols, sums_send, sums_recv, 3 * index))

    def end(index):
        cols = chunks[index]
        mean, scale = end_stats(sums[index], 4.0 * size)
        stats_ref[0:1, cols] = mean
        stats_ref[1:2, cols] = scale
        normed = (mid_ref[:, cols] - mean) * scale * par_ref[:, GAIN2 : GAIN2 + 1]
        h_ref[own, cols] = (normed + par_ref[:, SHIFT2 : SHIFT2 + 1]).astype(h_ref.dtype)
        gathers.append(ColGather(place, h_ref, cols, h_send, h_recv, 3 * index))
        gathers[-1].start()

    begin(0)
    end(0)
    gather.step(1)
    begin(1)
    end(1)
    gathers[0].forward()
    gather.step(2)
    gathers[1].forward()
    gather.step(3)
    for item in gathers:
        item.finish()
    gather.finish()


def turn_kernel(
    part_ref, mid_ref, cot_ref, stats_ref, par_ref, first_ref, second_ref,
    gx_ref, ga_ref, vec_ref, first_out, second_out,
    up_keep, slots, stage, stat, rs_send, rs_recv, sums_send, sums_recv, ga_send, ga_recv,
    *row_scratch,
):
    place = Place()
    greet(place, True)
    size = mid_ref.shape[0]
    rows = first_out.shape[0]
    everything = pl.ds(0, first_ref.shape[1])
    chunks = chunks_of(mid_ref.shape[1])
    own = pl.ds(pl.multiple_of(place.col * size, size), size)
    gain = par_ref[:, GAIN2 : GAIN2 + 1]
    scatters = [
        ColScatter(place, part_ref, slots, stage, cols, rs_send, rs_recv, 3 * index)
        for index, cols in enumerate(chunks)
    ]
    for item in scatters:
        item.start()
    summer = RowScatter(
        place, (first_ref, everything), (second_ref, everything), rows, *row_scratch
    )
    summer.start()
    for item in scatters:
        item.forward()
    summer.second_start()
    gathers = []

    def scaled(cols):
        return (mid_ref[:, cols] - stats_ref[0:1, cols]) * stats_ref[1:2, cols]

    def turn(index):
        cols = chunks[index]
        upstream = scatters[index].finish()
        up_keep[:, cols] = upstream
        xhat = scaled(cols)
        sums = begin_back(
            place, upstream, xhat, gain, stat, cols, sums_send, sums_recv, 3 * index
        )
        back = end_back(sums, upstream, xhat, stats_ref[1:2, cols], gain, 4.0 * size)
        gx = cot_ref[:, cols] + back
        gx_ref[:, cols] = gx
        ga_ref[own, cols] = gx.astype(ga_ref.dtype)
        gathers.append(ColGather(place, ga_ref, cols, ga_send, ga_recv, 3 * index))
        gathers[-1].start()

    turn(0)
    summer.third()
    turn(1)
    summer.fourth()
    gathers[0].forward()
    summer.fifth()
    gathers[1].forward()
    vec_ref[0:1, :] = token_sum(up_keep[...] * scaled(pl.ds(0, mid_ref.shape[1])))
    vec_ref[1:2, :] = token_sum(up_keep[...])
    for item in gathers:
        item.finish()
    summer.finish(first_out, second_out)


def leave_kernel(
    part_ref, out_part_ref, x_ref, mid_ref, stats_ref, par_ref, gx_ref, grads_ref, vec_ref,
    gin_ref, out_ref, first_out, second_out, vecs_ref,
    slots, stage, out_slots, out_stage, stat,
    rs_send, rs_recv, out_send, out_recv, sums_send, sums_recv,
    vec_slots, vec_send, vec_recv, *row_scratch,
):
    place = Place()
    greet(place, True)
    size = x_ref.shape[0]
    rows = first_out.shape[0]
    half = grads_ref.shape[1] // 2
    everything = pl.ds(0, x_ref.shape[1])
    gain = par_ref[:, GAIN1 : GAIN1 + 1]
    scatter = ColScatter(place, part_ref, slots, stage, everything, rs_send, rs_recv, 0)
    scatter.start()
    summer = RowScatter(
        place, (grads_ref, pl.ds(0, half)), (grads_ref, pl.ds(half, half)), rows, *row_scratch
    )
    summer.start()
    out_scatter = ColScatter(
        place, out_part_ref, out_slots, out_stage, everything, out_send, out_recv, 0
    )
    out_scatter.start()
    scatter.forward()
    out_scatter.forward()
    summer.second_start()
    summer.third()
    scale = stats_ref[1:2, :]
    upstream = scatter.finish()
    scaled = (x_ref[...] - stats_ref[0:1, :]) * scale
    sums = begin_back(place, upstream, scaled, gain, stat, everything, sums_send, sums_recv, 0)
    vec_slots[place.row] = vec_ref[...]
    vec_slots[place.row, 10:11, 0:size] = token_sum(upstream * scaled)
    vec_slots[place.row, 11:12, 0:size] = token_sum(upstream)
    vec_copies = []
    for step in range(1, 8):
        peer = lax.rem(place.row + step, 8)
        copy = remote(
            vec_slots.at[place.row],
            vec_slots.at[place.row],
            vec_send.at[step - 1],
            vec_recv.at[step - 1],
            {"row": peer},
        )
        copy.start()
        vec_copies.append(copy)
    summer.fourth()
    gin_ref[...] = gx_ref[...] + end_back(sums, upstream, scaled, scale, gain, 4.0 * size)
    summer.fifth()
    out_ref[...] = out_scatter.finish() + mid_ref[...] + par_ref[:, BIAS_FC2 : BIAS_FC2 + 1]
    summer.finish(first_out, second_out)
    for copy in vec_copies:
        copy.wait()
    total = vec_slots[0]
    for index in range(1, 8):
        total = total + vec_slots[index]
    vecs_ref[...] = total


def communicate(kernel, number, shapes, scratch, *operands):
    return pl.pallas_call(
        kernel,
        out_shape=[jax.ShapeDtypeStruct(*shape) for shape in shapes],
        in_specs=[pl.BlockSpec(memory_space=pltpu.VMEM)] * len(operands),
        out_specs=[pl.BlockSpec(memory_space=pltpu.VMEM)] * len(shapes),
        scratch_shapes=scratch,
        compiler_params=pltpu.CompilerParams(
            collective_id=number, has_side_effects=True, vmem_limit_bytes=VMEM_LIMIT
        ),
    )(*operands)


def sems(*counts):
    pairs = []
    for count in counts:
        pairs += [pltpu.SemaphoreType.DMA((count,)), pltpu.SemaphoreType.DMA((count,))]
    return pairs


def allowed_pairs(keys, start, width, key_seg, query_seg):
    key_pos = lax.broadcasted_iota(jnp.int32, (keys, width), 0)
    query_pos = lax.broadcasted_iota(jnp.int32, (keys, width), 1) + start
    return (key_seg == query_seg) & (key_pos <= query_pos)


def attend_kernel(q_ref, k_ref, v_ref, key_seg_ref, query_seg_ref, o_ref, log_ref):
    tokens = q_ref.shape[1]
    width = tokens // 4
    for start in range(0, tokens, width):
        keys = start + width
        mine = pl.ds(start, width)
        scores = left_product(k_ref[:, 0:keys], q_ref[:, mine])
        allowed = allowed_pairs(
            keys, start, width, key_seg_ref[0:keys, :], query_seg_ref[:, mine]
        )
        scores = jnp.where(allowed, scores, NEG)
        top = jnp.max(scores, axis=0, keepdims=True)
        expo = jnp.exp(scores - top)
        total = jnp.sum(expo, axis=0, keepdims=True)
        probs = (expo * (1.0 / total)).astype(jnp.bfloat16)
        o_ref[:, mine] = product(v_ref[:, 0:keys], probs).astype(o_ref.dtype)
        log_ref[0, :, mine] = top + jnp.log(total)


def attend_back_kernel(
    q_ref, k_ref, v_ref, go_ref, log_ref, key_seg_ref, query_seg_ref,
    gq_ref, gk_ref, gv_ref, gk_sum, gv_sum,
):
    tokens = q_ref.shape[1]
    width = tokens // 4
    gk_sum[...] = jnp.zeros_like(gk_sum)
    gv_sum[...] = jnp.zeros_like(gv_sum)
    for start in range(0, tokens, width):
        keys = start + width
        mine = pl.ds(start, width)
        queries, upstream = q_ref[:, mine], go_ref[:, mine]
        scores = left_product(k_ref[:, 0:keys], queries)
        allowed = allowed_pairs(
            keys, start, width, key_seg_ref[0:keys, :], query_seg_ref[:, mine]
        )
        probs = jnp.exp(jnp.where(allowed, scores, NEG) - log_ref[0, :, mine])
        grad_probs = left_product(v_ref[:, 0:keys], upstream)
        inner = jnp.sum(probs * grad_probs, axis=0, keepdims=True)
        grad_scores = (probs * (grad_probs - inner)).astype(jnp.bfloat16)
        grad_q = product(k_ref[:, 0:keys], grad_scores).astype(jnp.bfloat16)
        gq_ref[:, mine] = (grad_q.astype(jnp.float32) * HEAD_DIM ** (-0.5)).astype(gq_ref.dtype)
        gk_sum[:, 0:keys] += right_product(queries, grad_scores)
        gv_sum[:, 0:keys] += right_product(upstream, probs.astype(jnp.bfloat16))
    gk_ref[...] = gk_sum[...].astype(gk_ref.dtype)
    gv_ref[...] = gv_sum[...].astype(gv_ref.dtype)


def head_spec(tokens, offset):
    return pl.BlockSpec((HEAD_DIM, tokens), lambda head: (head + offset, 0))


def whole_spec(shape):
    return pl.BlockSpec(shape, lambda head: (0,) * len(shape))


def local_params():
    return pltpu.CompilerParams(vmem_limit_bytes=VMEM_LIMIT)


def attend(qkv, key_seg, query_seg):
    size, tokens = qkv.shape[0] // 3, qkv.shape[1]
    heads = size // HEAD_DIM
    log_spec = pl.BlockSpec((1, 1, tokens), lambda head: (head, 0, 0))
    return pl.pallas_call(
        attend_kernel,
        grid=(heads,),
        in_specs=[head_spec(tokens, part * heads) for part in range(3)]
        + [whole_spec((tokens, 1)), whole_spec((1, tokens))],
        out_specs=[head_spec(tokens, 0), log_spec],
        out_shape=[
            jax.ShapeDtypeStruct((size, tokens), jnp.bfloat16),
            jax.ShapeDtypeStruct((heads, 1, tokens), jnp.float32),
        ],
        compiler_params=local_params(),
    )(qkv, qkv, qkv, key_seg, query_seg)


def attend_back(qkv, grad_mixed, log_total, key_seg, query_seg):
    size, tokens = qkv.shape[0] // 3, qkv.shape[1]
    heads = size // HEAD_DIM
    log_spec = pl.BlockSpec((1, 1, tokens), lambda head: (head, 0, 0))
    return pl.pallas_call(
        attend_back_kernel,
        grid=(heads,),
        in_specs=[head_spec(tokens, part * heads) for part in range(3)]
        + [head_spec(tokens, 0), log_spec, whole_spec((tokens, 1)), whole_spec((1, tokens))],
        out_specs=[head_spec(tokens, 0)] * 3,
        out_shape=[jax.ShapeDtypeStruct((size, tokens), jnp.bfloat16)] * 3,
        scratch_shapes=[pltpu.VMEM((HEAD_DIM, tokens), jnp.float32)] * 2,
        compiler_params=local_params(),
    )(qkv, qkv, qkv, grad_mixed, log_total, key_seg, query_seg)


def fast_shards(
    layer_input,
    ln1_gain,
    ln1_bias,
    w_query,
    w_key,
    w_value,
    b_query,
    b_value,
    w_out,
    b_out,
    ln2_gain,
    ln2_bias,
    w_fc1,
    b_fc1,
    w_fc2,
    b_fc2,
    seq_lengths,
    cotangent,
):
    half, wide = jnp.bfloat16, jnp.float32
    size, tokens = layer_input.shape
    full = 4 * size
    rows, hidden_size = w_fc1.shape
    width = 4 * size + 2 * hidden_size
    scaling = HEAD_DIM ** (-0.5)
    places = jnp.arange(tokens, dtype=jnp.int32)
    ends = [seq_lengths[0, 0]]
    for index in range(1, 3):
        ends.append(ends[-1] + seq_lengths[0, index])
    segment = sum((places >= end).astype(jnp.int32) for end in ends)
    key_seg, query_seg = segment[:, None], segment[None, :]
    packed = jnp.concatenate([w_query, w_key, w_value, w_out.T], axis=1)
    params = jnp.stack([ln1_gain, ln1_bias, b_out, ln2_gain, ln2_bias, b_fc2], axis=1)
    stat = pltpu.VMEM((4, 8, tokens), wide)
    slots = pltpu.VMEM((3, size, tokens), half)
    stage = pltpu.VMEM((size, tokens), half)
    own_f32 = ((size, tokens), wide)
    all_half = ((full, tokens), half)
    stats_shape = ((8, tokens), wide)
    each = 3 * CHUNKS

    normed1, grad_mlp, stats1, weights = communicate(
        enter_kernel,
        1,
        [all_half, all_half, stats_shape, ((full, full), half)],
        [stat] + sems(each, each, each) + row_gather_scratch(),
        layer_input,
        cotangent,
        params,
        packed,
    )
    w_qkv, w_up = weights[:, : 3 * size], weights[:, 3 * size :]
    qkv_bias = jnp.concatenate([b_query, jnp.zeros_like(b_query), b_value])[:, None]
    qkv_scale = jnp.where(jnp.arange(3 * size) < size, scaling, 1.0)[:, None]
    qkv = to_half((left_product(w_qkv, normed1) + qkv_bias) * qkv_scale)
    mixed, log_total = attend(qkv, key_seg, query_seg)
    middle, normed2, stats2, w_first, w_second = communicate(
        middle_kernel,
        2,
        [own_f32, all_half, stats_shape] + [((8 * rows, hidden_size), half)] * 2,
        [slots, stage, stat] + sems(each, each, each) + row_gather_scratch(),
        to_half(product(w_up, mixed)),
        layer_input,
        params,
        w_fc1,
        w_fc2.T,
    )
    hidden_pre = left_product(w_first, normed2) + b_fc1[:, None]
    activated, gate_pull = jax.vjp(smooth_gate, hidden_pre)
    hidden = to_half(activated)
    grad_pre = to_half(gate_pull(left_product(w_second, grad_mlp))[0])
    grad_middle, grad_branch, norm2_sums, sum_first, sum_second = communicate(
        turn_kernel,
        3,
        [own_f32, all_half, ((8, size), wide)] + [((rows, hidden_size), wide)] * 2,
        [pltpu.VMEM((size, tokens), wide), slots, stage, stat]
        + sems(each, each, each)
        + row_scatter_scratch(rows, hidden_size, half, wide),
        to_half(product(w_first, grad_pre)),
        middle,
        cotangent,
        stats2,
        params,
        to_half(right_product(normed2, grad_pre)),
        to_half(right_product(grad_mlp, hidden)),
    )
    grad_mixed = to_half(left_product(w_up, grad_branch))
    grad_q, grad_k, grad_v = attend_back(qkv, grad_mixed, log_total, key_seg, query_seg)
    grad_qkv = jnp.concatenate([grad_q, grad_k, grad_v], axis=0)
    grads = jnp.concatenate(
        [
            to_half(right_product(normed1, grad_qkv)),
            to_half(right_product(grad_branch, mixed)),
        ],
        axis=1,
    )

    def along(values):
        return jnp.sum(values.astype(wide), axis=1)

    vectors = jnp.concatenate(
        [
            along(grad_q)[None],
            along(grad_v)[None],
            along(to_half(grad_middle))[None],
            norm2_sums[0:2],
            along(to_half(cotangent))[None],
            along(grad_pre).reshape(hidden_size // size, size),
            jnp.zeros((6, size), wide),
        ],
        axis=0,
    )
    vectors = jnp.pad(vectors, ((0, 0), (0, 256 - size)))
    grad_input, output, sum_qk, sum_vo, vector_sums = communicate(
        leave_kernel,
        4,
        [own_f32, own_f32] + [((rows, full // 2), wide)] * 2 + [(vectors.shape, wide)],
        [slots, stage, slots, stage, stat]
        + sems(3, 3, 3)
        + [pltpu.VMEM((8,) + vectors.shape, wide)]
        + sems(7)
        + row_scatter_scratch(rows, full // 2, half, wide),
        to_half(product(w_qkv, grad_qkv)),
        to_half(product(w_second, hidden)),
        layer_input,
        middle,
        stats1,
        params,
        grad_middle,
        grads,
        vectors,
    )
    vector_sums = vector_sums[:, :size]
    return (
        output,
        grad_input,
        vector_sums[10],
        vector_sums[11],
        sum_qk[:, :size],
        sum_qk[:, size:],
        sum_vo[:, :size],
        vector_sums[0],
        vector_sums[1],
        sum_vo[:, size:].T,
        vector_sums[2],
        vector_sums[3],
        vector_sums[4],
        sum_first,
        vector_sums[6:10].reshape(-1),
        sum_second.T,
        vector_sums[5],
    )


def solution(mesh):
    in_specs = (
        P("col", "row"),
        P("col"),
        P("col"),
        P("row", "col"),
        P("row", "col"),
        P("row", "col"),
        P("col"),
        P("col"),
        P("col", "row"),
        P("col"),
        P("col"),
        P("col"),
        P("row", "col"),
        P("col"),
        P("col", "row"),
        P("col"),
        P("row", None),
        P("col", "row"),
    )
    out_specs = (
        P("col", "row"),
        P("col", "row"),
        P("col"),
        P("col"),
        P("row", "col"),
        P("row", "col"),
        P("row", "col"),
        P("col"),
        P("col"),
        P("col", "row"),
        P("col"),
        P("col"),
        P("col"),
        P("row", "col"),
        P("col"),
        P("col", "row"),
        P("col"),
    )
    fits = mesh.shape["col"] == 4 and mesh.shape["row"] == 8
    body = fast_shards if fits else shards
    return jax.shard_map(body, mesh=mesh, in_specs=in_specs, out_specs=out_specs, check_vma=False)
```

```python
import functools

import jax
import jax.numpy as jnp
from jax import lax
from jax.experimental import pallas as pl
from jax.experimental.pallas import tpu as pltpu
from jax.sharding import PartitionSpec as P

HEADS = 12
HEAD_DIM = 64


EPS = 1e-05
NEG = -1e30


def to_half(values):
    return values.astype(jnp.bfloat16)


def product(first_op, second_op):
    return jnp.dot(first_op, second_op, preferred_element_type=jnp.float32)


def product_left(first_op, second_op):
    return lax.dot_general(
        first_op, second_op, (((0,), (0,)), ((), ())), preferred_element_type=jnp.float32
    )


def product_right(first_op, second_op):
    return lax.dot_general(
        first_op, second_op, (((1,), (1,)), ((), ())), preferred_element_type=jnp.float32
    )


def column_sum(values):
    return jnp.sum(values.astype(jnp.float32), axis=0)


def smooth_gate(values):
    return jax.nn.gelu(values, approximate=True)


def query_positions(pack_rows):
    col_count = lax.axis_size("col")
    col_index = lax.axis_index("col")
    share_rows = pack_rows // col_count
    return col_index * share_rows + jnp.arange(share_rows, dtype=jnp.int32)


def feature_rows(block_rows):
    return lax.all_gather(block_rows, "col", axis=1, tiled=True)


def feature_sums(partial_value):
    return lax.psum_scatter(partial_value, "col", scatter_dimension=1, tiled=True)


def to_heads(block_rows):
    return lax.all_to_all(block_rows, "col", split_axis=0, concat_axis=1, tiled=True)


def to_features(block_rows):
    spread = lax.all_to_all(block_rows, "col", split_axis=1, concat_axis=0, tiled=True)
    return spread


def norm_forward(block_rows, norm_gain, norm_shift):
    local_width = block_rows.shape[1]
    full_width = local_width * lax.axis_size("col")
    row_sums, row_squares = lax.psum(
        (jnp.sum(block_rows, axis=1), jnp.sum(block_rows * block_rows, axis=1)), "col"
    )
    row_mean = (row_sums / full_width)[:, None]
    variance = (row_squares / full_width)[:, None] - row_mean * row_mean
    row_scale = lax.rsqrt(variance + EPS)
    scaled = (block_rows - row_mean) * row_scale
    normed = feature_rows(to_half(scaled * norm_gain + norm_shift))
    return (normed, scaled, row_scale)


def norm_backward(upstream, scaled, row_scale, norm_gain):
    full_width = upstream.shape[1] * lax.axis_size("col")
    weighted = upstream * norm_gain
    row_sums, row_along = lax.psum(
        (jnp.sum(weighted, axis=1), jnp.sum(weighted * scaled, axis=1)), "col"
    )
    grad_rows = row_scale * (
        weighted - (row_sums / full_width)[:, None] - scaled * (row_along / full_width)[:, None]
    )
    return (grad_rows, jnp.sum(upstream * scaled, axis=0), jnp.sum(upstream, axis=0))


def split_heads(block_rows):
    return block_rows.reshape(block_rows.shape[0], HEADS, HEAD_DIM)


def masked_scores(queries, all_keys, query_pos, segment):
    scores = jnp.einsum(
        "qhd,khd->hqk",
        split_heads(queries),
        split_heads(all_keys),
        preferred_element_type=jnp.float32,
    )
    key_pos = jnp.arange(all_keys.shape[0], dtype=jnp.int32)
    allowed = (segment[query_pos][:, None] == segment[None, :]) & (
        key_pos[None, :] <= query_pos[:, None]
    )
    return jnp.where(allowed[None], scores, NEG)


def attention_forward(queries, all_keys, all_values, query_pos, segment):
    scores = masked_scores(queries, all_keys, query_pos, segment)
    row_top = jnp.max(scores, axis=2, keepdims=True)
    expo_vals = jnp.exp(scores - row_top)
    row_total = jnp.sum(expo_vals, axis=2, keepdims=True)
    attn_probs = to_half(expo_vals / row_total)
    mixed = jnp.einsum(
        "hqk,khd->qhd", attn_probs, split_heads(all_values), preferred_element_type=jnp.float32
    )
    return (mixed.reshape(queries.shape[0], -1), row_top + jnp.log(row_total))


def attention_backward(queries, all_keys, all_values, query_pos, segment, log_total, grad_mixed):
    scores = masked_scores(queries, all_keys, query_pos, segment)
    attn_probs = jnp.exp(scores - log_total)
    grad_heads = split_heads(grad_mixed)
    grad_probs = jnp.einsum(
        "qhd,khd->hqk", grad_heads, split_heads(all_values), preferred_element_type=jnp.float32
    )
    row_inner = jnp.sum(attn_probs * grad_probs, axis=2, keepdims=True)
    grad_scores = to_half(attn_probs * (grad_probs - row_inner))
    grad_queries = jnp.einsum(
        "hqk,khd->qhd", grad_scores, split_heads(all_keys), preferred_element_type=jnp.float32
    )
    grad_keys = jnp.einsum(
        "hqk,qhd->khd", grad_scores, split_heads(queries), preferred_element_type=jnp.float32
    )
    grad_values = jnp.einsum(
        "hqk,qhd->khd", to_half(attn_probs), grad_heads, preferred_element_type=jnp.float32
    )
    key_count = all_keys.shape[0]
    return (
        grad_queries.reshape(queries.shape[0], -1),
        grad_keys.reshape(key_count, -1),
        grad_values.reshape(key_count, -1),
    )


def shards(
    layer_input,
    ln1_gain,
    ln1_bias,
    w_query,
    w_key,
    w_value,
    b_query,
    b_value,
    w_out,
    b_out,
    ln2_gain,
    ln2_bias,
    w_fc1,
    b_fc1,
    w_fc2,
    b_fc2,
    seq_lengths,
    cotangent,
):
    scaling = HEAD_DIM ** (-0.5)
    input_rows = layer_input.T
    cotangent_rows = cotangent.T
    pack_rows = input_rows.shape[0]
    seq_ends = jnp.cumsum(seq_lengths[0])
    places = jnp.arange(pack_rows, dtype=jnp.int32)
    segment = jnp.sum((places[:, None] >= seq_ends[None, :]).astype(jnp.int32), axis=1)
    query_pos = query_positions(pack_rows)
    gathered = (
        lax.all_gather(w_query, "row", axis=0, tiled=True),
        lax.all_gather(w_key, "row", axis=0, tiled=True),
        lax.all_gather(w_value, "row", axis=0, tiled=True),
        lax.all_gather(w_fc1, "row", axis=0, tiled=True),
        lax.all_gather(w_out.T, "row", axis=0, tiled=True),
        lax.all_gather(w_fc2.T, "row", axis=0, tiled=True),
    )
    full_query, full_key, full_value, full_fc1, full_out, full_fc2 = gathered
    normed1, scaled1, scale1 = norm_forward(input_rows, ln1_gain, ln1_bias)
    query_part = to_half((product(normed1, full_query) + b_query) * scaling)
    key_part = to_half(product(normed1, full_key))
    value_part = to_half(product(normed1, full_value) + b_value)
    queries = to_heads(query_part)
    all_keys, all_values = (
        lax.all_gather(key_part, "col", axis=1, tiled=True),
        lax.all_gather(value_part, "col", axis=1, tiled=True),
    )
    attended, log_total = attention_forward(queries, all_keys, all_values, query_pos, segment)
    spread = to_features(to_half(attended))
    middle = input_rows + feature_sums(product_right(spread, full_out)) + b_out
    normed2, scaled2, scale2 = norm_forward(middle, ln2_gain, ln2_bias)
    hidden_pre = product(normed2, full_fc1) + b_fc1
    activated, gate_pull = jax.vjp(smooth_gate, hidden_pre)
    hidden = to_half(activated)
    output = middle + feature_sums(product_right(hidden, full_fc2)) + b_fc2
    grad_mlp = to_half(cotangent_rows)
    grad_mlp_full = feature_rows(grad_mlp)
    grad_hidden = product(grad_mlp_full, full_fc2)
    grad_pre = to_half(gate_pull(grad_hidden)[0])
    grad_fc2_t = product_left(grad_mlp_full, hidden)
    grad_fc1 = product_left(normed2, grad_pre)
    grad_normed2 = feature_sums(product_right(grad_pre, full_fc1))
    back_second, gain2_grad, shift2_grad = norm_backward(grad_normed2, scaled2, scale2, ln2_gain)
    grad_middle = cotangent_rows + back_second
    grad_branch = to_half(grad_middle)
    grad_branch_full = feature_rows(grad_branch)
    grad_out_t = product_left(grad_branch_full, spread)
    grad_spread = to_half(product(grad_branch_full, full_out))
    grad_attended = to_heads(grad_spread)
    grad_q_heads, grad_k_part, grad_v_part = attention_backward(
        queries, all_keys, all_values, query_pos, segment, log_total, grad_attended
    )
    grad_query_raw = to_features(to_half(grad_q_heads)).astype(jnp.float32) * scaling
    grad_query = to_half(grad_query_raw)
    key_total, value_total = (
        lax.psum_scatter(
            grad_k_part.astype(jnp.bfloat16), "col", scatter_dimension=1, tiled=True
        ).astype(jnp.float32),
        lax.psum_scatter(
            grad_v_part.astype(jnp.bfloat16), "col", scatter_dimension=1, tiled=True
        ).astype(jnp.float32),
    )
    grad_key = to_half(key_total)
    grad_value = to_half(value_total)
    grad_normed1 = feature_sums(
        product_right(grad_query, full_query)
        + product_right(grad_key, full_key)
        + product_right(grad_value, full_value)
    )
    back_first, gain1_grad, shift1_grad = norm_backward(grad_normed1, scaled1, scale1, ln1_gain)
    grad_input = grad_middle + back_first
    weight_sums = (
        lax.psum_scatter(
            product_left(normed1, grad_query).astype(jnp.bfloat16),
            "row",
            scatter_dimension=0,
            tiled=True,
        ).astype(jnp.float32),
        lax.psum_scatter(
            product_left(normed1, grad_key).astype(jnp.bfloat16),
            "row",
            scatter_dimension=0,
            tiled=True,
        ).astype(jnp.float32),
        lax.psum_scatter(
            product_left(normed1, grad_value).astype(jnp.bfloat16),
            "row",
            scatter_dimension=0,
            tiled=True,
        ).astype(jnp.float32),
        lax.psum_scatter(
            grad_out_t.astype(jnp.bfloat16), "row", scatter_dimension=0, tiled=True
        ).astype(jnp.float32),
        lax.psum_scatter(
            grad_fc1.astype(jnp.bfloat16), "row", scatter_dimension=0, tiled=True
        ).astype(jnp.float32),
        lax.psum_scatter(
            grad_fc2_t.astype(jnp.bfloat16), "row", scatter_dimension=0, tiled=True
        ).astype(jnp.float32),
    )
    vector_sums = lax.psum(
        (
            gain1_grad,
            shift1_grad,
            column_sum(grad_query_raw),
            column_sum(grad_value),
            column_sum(grad_branch),
            gain2_grad,
            shift2_grad,
            column_sum(grad_pre),
            column_sum(grad_mlp),
        ),
        "row",
    )
    return (
        output.T,
        grad_input.T,
        vector_sums[0],
        vector_sums[1],
        weight_sums[0],
        weight_sums[1],
        weight_sums[2],
        vector_sums[2],
        vector_sums[3],
        weight_sums[3].T,
        vector_sums[4],
        vector_sums[5],
        vector_sums[6],
        weight_sums[4],
        vector_sums[7],
        weight_sums[5].T,
        vector_sums[8],
    )


VMEM_LIMIT = 56 * 1024 * 1024
MESH_IDS = pl.DeviceIdType.MESH


def left_product(first_op, second_op, **extra):
    return lax.dot_general(
        first_op, second_op, (((0,), (0,)), ((), ())), preferred_element_type=jnp.float32, **extra
    )


def right_product(first_op, second_op, **extra):
    return lax.dot_general(
        first_op, second_op, (((1,), (1,)), ((), ())), preferred_element_type=jnp.float32, **extra
    )


def remote(source, target, send_sem, recv_sem, device):
    return pltpu.make_async_remote_copy(
        src_ref=source,
        dst_ref=target,
        send_sem=send_sem,
        recv_sem=recv_sem,
        device_id=device,
        device_id_type=MESH_IDS,
    )


class Place:
    def __init__(self):
        self.col = lax.axis_index("col")
        self.row = lax.axis_index("row")
        self.core_peer = self.col + 1 - 2 * lax.rem(self.col, 2)
        self.chip_peer = lax.rem(self.col + 2, 4)
        self.far_peer = lax.rem(self.core_peer + 2, 4)
        self.z = self.row // 2
        self.y = lax.rem(self.row, 2)
        self.y_peer = self.row + 1 - 2 * self.y


def greet(place, rows_too):
    barrier = pltpu.get_barrier_semaphore()
    count = 3
    for step in range(1, 4):
        peer = lax.rem(place.col + step, 4)
        pl.semaphore_signal(barrier, inc=1, device_id={"col": peer}, device_id_type=MESH_IDS)
    if rows_too:
        count += 7
        for step in range(1, 8):
            peer = lax.rem(place.row + step, 8)
            pl.semaphore_signal(barrier, inc=1, device_id={"row": peer}, device_id_type=MESH_IDS)
    pl.semaphore_wait(barrier, count)


class ColGather:
    def __init__(self, place, buf, columns, send, recv, base):
        self.place, self.buf, self.columns = place, buf, columns
        self.send, self.recv, self.base = send, recv, base
        self.size = buf.shape[0] // 4

    def block(self, index):
        rows = pl.ds(pl.multiple_of(index * self.size, self.size), self.size)
        return self.buf.at[rows, self.columns]

    def move(self, slot, source, device):
        slot += self.base
        return remote(source, source, self.send.at[slot], self.recv.at[slot], {"col": device})

    def start(self):
        own = self.block(self.place.col)
        self.chip = self.move(0, own, self.place.chip_peer)
        self.core = self.move(1, own, self.place.core_peer)
        self.chip.start()
        self.core.start()

    def forward(self):
        self.chip.wait_recv()
        got = self.block(self.place.chip_peer)
        self.onward = self.move(2, got, self.place.core_peer)
        self.onward.start()

    def finish(self):
        self.chip.wait_send()
        self.core.wait()
        self.onward.wait()


class ColScatter:
    def __init__(self, place, part, slots, stage, columns, send, recv, base):
        self.place, self.part, self.columns = place, part, columns
        self.slots, self.stage = slots, stage
        self.send, self.recv, self.base = send, recv, base
        self.size = part.shape[0] // 4

    def block(self, index):
        rows = pl.ds(pl.multiple_of(index * self.size, self.size), self.size)
        return self.part.at[rows, self.columns]

    def slot(self, index):
        return self.slots.at[index, :, self.columns]

    def move(self, slot, source, device):
        sem = slot + self.base
        return remote(
            source, self.slot(slot), self.send.at[sem], self.recv.at[sem], {"col": device}
        )

    def start(self):
        place = self.place
        self.far = self.move(0, self.block(place.far_peer), place.core_peer)
        self.far.start()
        self.near = self.move(1, self.block(place.core_peer), place.core_peer)
        self.near.start()

    def forward(self):
        self.far.wait_recv()
        mixed = self.block(self.place.chip_peer)[...].astype(jnp.float32) + self.slot(0)[
            ...
        ].astype(jnp.float32)
        staged = self.stage.at[:, self.columns]
        staged[...] = mixed.astype(self.stage.dtype)
        self.cross = self.move(2, staged, self.place.chip_peer)
        self.cross.start()

    def finish(self):
        self.far.wait_send()
        self.near.wait()
        self.cross.wait()
        own = self.block(self.place.col)[...].astype(jnp.float32)
        return own + self.slot(1)[...].astype(jnp.float32) + self.slot(2)[...].astype(jnp.float32)


class ColSums:
    def __init__(self, place, first, second, stat, columns, send, recv, base):
        self.stat, self.columns = stat, columns
        stat[place.col, 0:1, columns] = first
        stat[place.col, 1:2, columns] = second
        own = stat.at[place.col, :, columns]
        self.copies = []
        for step in range(1, 4):
            peer = lax.rem(place.col + step, 4)
            sem = base + step - 1
            copy = remote(own, own, send.at[sem], recv.at[sem], {"col": peer})
            copy.start()
            self.copies.append(copy)

    def finish(self):
        for copy in self.copies:
            copy.wait()
        part = [self.stat[index, :, self.columns] for index in range(4)]
        total = part[0] + part[1] + part[2] + part[3]
        return total[0:1], total[1:2]


def begin_stats(place, values, *rest):
    return ColSums(
        place,
        jnp.sum(values, axis=0, keepdims=True),
        jnp.sum(values * values, axis=0, keepdims=True),
        *rest,
    )


def end_stats(sums, width):
    total, squares = sums.finish()
    mean = total / width
    return mean, lax.rsqrt(squares / width - mean * mean + EPS)


def begin_back(place, upstream, scaled, gain, *rest):
    weighted = upstream * gain
    return ColSums(
        place,
        jnp.sum(weighted, axis=0, keepdims=True),
        jnp.sum(weighted * scaled, axis=0, keepdims=True),
        *rest,
    )


def end_back(sums, upstream, scaled, scale, gain, width):
    total, along = sums.finish()
    return scale * (upstream * gain - total / width - scaled * (along / width))


def token_sum(values):
    ones = jnp.ones((8, values.shape[1]), jnp.float32)
    return right_product(ones, values, precision=lax.Precision.HIGHEST)[0:1]


class LineGather:
    def __init__(self, place, buf, columns, size, stride, offset, send, recv, onward=None):
        self.place, self.buf, self.columns, self.size = place, buf, columns, size
        self.stride, self.offset, self.send, self.recv = stride, offset, send, recv
        self.onward = onward

    def copy(self, hop, way):
        source = self.place.z - way * hop
        start = pl.multiple_of(jnp.clip(source, 0, 3) * self.stride + self.offset, 16)
        block = self.buf.at[pl.ds(start, self.size), self.columns]
        slot = 4 * (1 if way < 0 else 0)
        target = jnp.clip(self.place.row + 2 * way, 0, 7)
        return remote(
            block, block, self.send.at[slot + hop], self.recv.at[slot + hop + 1], {"row": target}
        )

    def arrived(self, hop, way):
        slot = 4 * (1 if way < 0 else 0)
        start = pl.multiple_of(
            jnp.clip(self.place.z - way * hop, 0, 3) * self.stride + self.offset, 16
        )
        block = self.buf.at[pl.ds(start, self.size), self.columns]
        pltpu.make_async_copy(block, block, self.recv.at[slot + hop]).wait()

    def has(self, hop, way):
        return self.place.z >= hop if way > 0 else self.place.z + hop <= 3

    def sends(self, hop, way):
        more = self.place.z < 3 if way > 0 else self.place.z > 0
        return jnp.logical_and(self.has(hop, way), more)

    def start(self):
        for way in (1, -1):

            @pl.when(self.sends(0, way))
            def _():
                self.copy(0, way).start()

    def step(self, hop):
        for way in (1, -1):

            @pl.when(self.has(hop, way))
            def _():
                self.arrived(hop, way)
                if self.onward is not None:
                    self.onward(hop, way).start()

            if hop < 3:

                @pl.when(self.sends(hop, way))
                def _():
                    self.copy(hop, way).start()

    def finish(self):
        if self.onward is not None:
            for hop in range(1, 4):
                for way in (1, -1):

                    @pl.when(self.has(hop, way))
                    def _():
                        self.onward(hop, way).wait()

        for hop in range(3):
            for way in (1, -1):

                @pl.when(self.sends(hop, way))
                def _():
                    self.copy(hop, way).wait_send()


class LineScatter:
    def __init__(self, place, block, right, left, send, recv):
        self.place, self.block, self.right, self.left = place, block, right, left
        self.send, self.recv = send, recv

    def copy(self, target_z, way):
        slots = self.right if way > 0 else self.left
        base = 0 if way > 0 else 4
        device = {"row": jnp.clip(self.place.row + 2 * way, 0, 7)}
        return remote(
            slots.at[target_z],
            slots.at[target_z],
            self.send.at[base + target_z],
            self.recv.at[base + target_z],
            device,
        )

    def step(self, index):
        z = self.place.z
        for way, target_z in ((1, 3 - index), (-1, index)):
            slots = self.right if way > 0 else self.left
            relays = z < target_z if way > 0 else z > target_z
            edge = z == 0 if way > 0 else z == 3
            inner = z > 0 if way > 0 else z < 3

            @pl.when(jnp.logical_and(relays, edge))
            def _():
                slots[target_z] = self.block(target_z)[...]

            @pl.when(jnp.logical_and(relays, inner))
            def _():
                self.copy(target_z, way).wait_recv()
                mixed = slots[target_z].astype(jnp.float32) + self.block(target_z)[...].astype(
                    jnp.float32
                )
                slots[target_z] = mixed.astype(slots.dtype)

            @pl.when(relays)
            def _():
                self.copy(target_z, way).start()

    def finish(self, total):
        z = self.place.z
        for target_z in range(4):

            @pl.when(z == target_z)
            def _():
                total[...] = self.block(target_z)[...].astype(jnp.float32)
                if target_z > 0:
                    self.copy(target_z, 1).wait_recv()
                    total[...] += self.right[target_z].astype(jnp.float32)
                if target_z < 3:
                    self.copy(target_z, -1).wait_recv()
                    total[...] += self.left[target_z].astype(jnp.float32)

            if target_z > 0:

                @pl.when(z < target_z)
                def _():
                    self.copy(target_z, 1).wait_send()

            if target_z < 3:

                @pl.when(z > target_z)
                def _():
                    self.copy(target_z, -1).wait_send()


def row_gather_scratch():
    return sems(8, 8, 8)


class RowGather:
    def __init__(self, place, first, second, rows, send_a, recv_a, send_b, recv_b, y_send, y_recv):
        self.place, self.rows = place, rows
        self.first, self.first_columns = first
        self.second, self.second_columns = second
        self.y_send, self.y_recv = y_send, y_recv
        self.line_a = LineGather(
            place, self.first, self.first_columns, rows, 2 * rows, place.y * rows,
            send_a, recv_a, self.onward,
        )
        self.line_b = LineGather(
            place, self.second, self.second_columns, 2 * rows, 2 * rows, 0, send_b, recv_b
        )

    def across(self, buf, columns, source_z, slot):
        start = pl.multiple_of(source_z * 2 * self.rows + self.place.y * self.rows, self.rows)
        block = buf.at[pl.ds(start, self.rows), columns]
        peer = {"row": self.place.y_peer}
        return remote(block, block, self.y_send.at[slot], self.y_recv.at[slot], peer)

    def onward(self, hop, way):
        source = jnp.clip(self.place.z - way * hop, 0, 3)
        slot = hop if way > 0 else hop + 3
        return self.across(self.first, self.first_columns, source, slot)

    def start(self):
        self.pair = self.across(self.second, self.second_columns, self.place.z, 7)
        self.pair.start()
        self.line_a.start()

    def second_start(self):
        self.pair.wait()
        self.line_b.start()
        self.mine = self.onward(0, 1)
        self.mine.start()

    def step(self, hop):
        self.line_a.step(hop)
        self.line_b.step(hop)

    def finish(self):
        self.mine.wait()
        self.line_a.finish()
        self.line_b.finish()


def row_scatter_scratch(rows, columns, half, wide):
    return (
        [pltpu.VMEM((4, rows, columns), half)] * 3
        + [pltpu.VMEM((4, 2 * rows, columns), half)] * 2
        + [
            pltpu.VMEM((2 * rows, columns), wide),
            pltpu.VMEM((rows, columns), half),
            pltpu.VMEM((rows, columns), half),
        ]
        + sems(5, 8, 8)
    )


class RowScatter:
    def __init__(
        self, place, first, second, rows, slots, right_a, left_a, right_b, left_b,
        total, stage, last, y_send, y_recv, send_a, recv_a, send_b, recv_b,
    ):
        self.place, self.rows, self.slots = place, rows, slots
        self.first, self.first_columns = first
        self.second, self.second_columns = second
        self.total, self.stage, self.last = total, stage, last
        self.y_send, self.y_recv = y_send, y_recv
        self.line_a = LineScatter(place, lambda k: slots.at[k], right_a, left_a, send_a, recv_a)
        self.line_b = LineScatter(
            place,
            lambda k: self.second.at[pl.ds(k * 2 * rows, 2 * rows), self.second_columns],
            right_b, left_b, send_b, recv_b,
        )

    def block(self, target_z, target_y):
        start = pl.multiple_of(target_z * 2 * self.rows + target_y * self.rows, self.rows)
        return self.first.at[pl.ds(start, self.rows), self.first_columns]

    def start(self):
        self.copies = {}
        for target_z in (3, 0, 2, 1):
            self.copies[target_z] = remote(
                self.block(target_z, 1 - self.place.y),
                self.slots.at[target_z],
                self.y_send.at[target_z],
                self.y_recv.at[target_z],
                {"row": self.place.y_peer},
            )
            self.copies[target_z].start()
        self.line_b.step(0)

    def mix(self, target_z):
        self.copies[target_z].wait()
        mixed = self.slots[target_z].astype(jnp.float32) + self.block(target_z, self.place.y)[
            ...
        ].astype(jnp.float32)
        self.slots[target_z] = mixed.astype(self.slots.dtype)

    def second_start(self):
        self.mix(3)
        self.mix(0)
        self.line_a.step(0)
        self.mix(2)
        self.mix(1)

    def third(self):
        self.line_b.step(1)
        self.line_a.step(1)

    def fourth(self):
        self.line_b.step(2)
        self.line_a.step(2)

    def fifth(self):
        rows = self.rows
        self.line_b.finish(self.total)
        theirs = pl.ds(pl.multiple_of((1 - self.place.y) * rows, rows), rows)
        self.stage[...] = self.total[theirs, :].astype(self.stage.dtype)
        self.final = remote(
            self.stage, self.last, self.y_send.at[4], self.y_recv.at[4], {"row": self.place.y_peer}
        )
        self.final.start()

    def finish(self, first_out, second_out):
        rows = self.rows
        self.line_a.finish(first_out)
        self.final.wait()
        ours = pl.ds(pl.multiple_of(self.place.y * rows, rows), rows)
        second_out[...] = self.total[ours, :] + self.last[...].astype(jnp.float32)


CHUNKS = 2


def chunks_of(tokens):
    width = tokens // CHUNKS
    return [pl.ds(index * width, width) for index in range(CHUNKS)]


GAIN1, SHIFT1, BIAS_OUT, GAIN2, SHIFT2, BIAS_FC2 = range(6)


def enter_kernel(
    x_ref, par_ref, wq_ref, wk_ref, wv_ref, wo_ref,
    h_ref, stats_ref, full_ref,
    stat, sums_send, sums_recv, h_send, h_recv, *row_scratch,
):
    place = Place()
    greet(place, True)
    size = x_ref.shape[0]
    rows = wq_ref.shape[0]
    half = 2 * size
    chunks = chunks_of(x_ref.shape[1])
    own = pl.ds(pl.multiple_of(place.col * size, size), size)
    own_rows = pl.ds(pl.multiple_of(place.row * rows, rows), rows)
    for index, ref in enumerate((wq_ref, wk_ref, wv_ref, wo_ref)):
        full_ref[own_rows, index * size : (index + 1) * size] = ref[...]
    gather = RowGather(
        place, (full_ref, pl.ds(0, half)), (full_ref, pl.ds(half, half)), rows, *row_scratch
    )
    gather.start()
    sums = [
        begin_stats(place, x_ref[:, cols], stat, cols, sums_send, sums_recv, 3 * index)
        for index, cols in enumerate(chunks)
    ]
    gathers = []
    for index, cols in enumerate(chunks):
        mean, scale = end_stats(sums[index], 4.0 * size)
        stats_ref[0:1, cols] = mean
        stats_ref[1:2, cols] = scale
        normed = (x_ref[:, cols] - mean) * scale * par_ref[:, GAIN1 : GAIN1 + 1]
        h_ref[own, cols] = (normed + par_ref[:, SHIFT1 : SHIFT1 + 1]).astype(h_ref.dtype)
        gathers.append(ColGather(place, h_ref, cols, h_send, h_recv, 3 * index))
        gathers[-1].start()
    gather.second_start()
    gather.step(1)
    gathers[0].forward()
    gather.step(2)
    gathers[1].forward()
    gather.step(3)
    for item in gathers:
        item.finish()
    gather.finish()


def middle_kernel(
    part_ref, x_ref, cot_ref, par_ref, first_ref, second_ref,
    mid_ref, h_ref, gm_ref, stats_ref, full_first, full_second,
    slots, stage, stat, rs_send, rs_recv, sums_send, sums_recv, h_send, h_recv,
    gm_send, gm_recv, *row_scratch,
):
    place = Place()
    greet(place, True)
    size = x_ref.shape[0]
    rows, columns = first_ref.shape
    chunks = chunks_of(x_ref.shape[1])
    own = pl.ds(pl.multiple_of(place.col * size, size), size)
    scatters = [
        ColScatter(place, part_ref, slots, stage, cols, rs_send, rs_recv, 3 * index)
        for index, cols in enumerate(chunks)
    ]
    for item in scatters:
        item.start()
    own_rows = pl.ds(pl.multiple_of(place.row * rows, rows), rows)
    full_first[own_rows, :] = first_ref[...]
    full_second[own_rows, :] = second_ref[...]
    everything = pl.ds(0, columns)
    gather = RowGather(
        place, (full_first, everything), (full_second, everything), rows, *row_scratch
    )
    gather.start()
    for item in scatters:
        item.forward()
    gm_ref[own, :] = cot_ref[...].astype(gm_ref.dtype)
    gather.second_start()
    sums, gathers = [], []

    def begin(index):
        cols = chunks[index]
        values = scatters[index].finish() + x_ref[:, cols] + par_ref[:, BIAS_OUT : BIAS_OUT + 1]
        mid_ref[:, cols] = values
        sums.append(begin_stats(place, values, stat, cols, sums_send, sums_recv, 3 * index))

    def end(index):
        cols = chunks[index]
        mean, scale = end_stats(sums[index], 4.0 * size)
        stats_ref[0:1, cols] = mean
        stats_ref[1:2, cols] = scale
        normed = (mid_ref[:, cols] - mean) * scale * par_ref[:, GAIN2 : GAIN2 + 1]
        h_ref[own, cols] = (normed + par_ref[:, SHIFT2 : SHIFT2 + 1]).astype(h_ref.dtype)
        gathers.append(ColGather(place, h_ref, cols, h_send, h_recv, 3 * index))
        gathers[-1].start()

    begin(0)
    end(0)
    gather.step(1)
    begin(1)
    end(1)
    everywhere = pl.ds(0, x_ref.shape[1])
    gathers.append(ColGather(place, gm_ref, everywhere, gm_send, gm_recv, 0))
    gathers[2].start()
    gathers[0].forward()
    gather.step(2)
    gathers[1].forward()
    gather.step(3)
    gathers[2].forward()
    for item in gathers:
        item.finish()
    gather.finish()


def turn_kernel(
    part_ref, out_part_ref, mid_ref, cot_ref, stats_ref, par_ref, first_ref, second_ref,
    gx_ref, ga_ref, out_ref, vec_ref, first_out, second_out,
    up_keep, slots, stage, out_slots, out_stage, stat, rs_send, rs_recv, out_send, out_recv, sums_send, sums_recv, ga_send, ga_recv,
    *row_scratch,
):
    place = Place()
    greet(place, True)
    size = mid_ref.shape[0]
    rows = first_out.shape[0]
    everything = pl.ds(0, first_ref.shape[1])
    chunks = chunks_of(mid_ref.shape[1])
    own = pl.ds(pl.multiple_of(place.col * size, size), size)
    gain = par_ref[:, GAIN2 : GAIN2 + 1]
    scatters = [
        ColScatter(place, part_ref, slots, stage, cols, rs_send, rs_recv, 3 * index)
        for index, cols in enumerate(chunks)
    ]
    for item in scatters:
        item.start()
    summer = RowScatter(
        place, (first_ref, everything), (second_ref, everything), rows, *row_scratch
    )
    summer.start()
    out_scatter = ColScatter(
        place, out_part_ref, out_slots, out_stage, pl.ds(0, mid_ref.shape[1]), out_send, out_recv, 0
    )
    out_scatter.start()
    for item in scatters:
        item.forward()
    summer.second_start()
    gathers = []

    def scaled(cols):
        return (mid_ref[:, cols] - stats_ref[0:1, cols]) * stats_ref[1:2, cols]

    def turn(index):
        cols = chunks[index]
        upstream = scatters[index].finish()
        up_keep[:, cols] = upstream
        xhat = scaled(cols)
        sums = begin_back(
            place, upstream, xhat, gain, stat, cols, sums_send, sums_recv, 3 * index
        )
        back = end_back(sums, upstream, xhat, stats_ref[1:2, cols], gain, 4.0 * size)
        gx = cot_ref[:, cols] + back
        gx_ref[:, cols] = gx
        ga_ref[own, cols] = gx.astype(ga_ref.dtype)
        gathers.append(ColGather(place, ga_ref, cols, ga_send, ga_recv, 3 * index))
        gathers[-1].start()

    turn(0)
    summer.third()
    turn(1)
    out_scatter.forward()
    summer.fourth()
    gathers[0].forward()
    summer.fifth()
    gathers[1].forward()
    vec_ref[0:1, :] = token_sum(up_keep[...] * scaled(pl.ds(0, mid_ref.shape[1])))
    vec_ref[1:2, :] = token_sum(up_keep[...])
    for item in gathers:
        item.finish()
    out_ref[...] = out_scatter.finish() + mid_ref[...] + par_ref[:, BIAS_FC2 : BIAS_FC2 + 1]
    summer.finish(first_out, second_out)


def leave_kernel(
    part_ref, x_ref, stats_ref, par_ref, gx_ref, grads_ref, vec_ref,
    gin_ref, first_out, second_out, vecs_ref,
    slots, stage, stat, rs_send, rs_recv, sums_send, sums_recv,
    vec_slots, vec_send, vec_recv, *row_scratch,
):
    place = Place()
    greet(place, True)
    size = x_ref.shape[0]
    rows = first_out.shape[0]
    half = grads_ref.shape[1] // 2
    everything = pl.ds(0, x_ref.shape[1])
    gain = par_ref[:, GAIN1 : GAIN1 + 1]
    scatter = ColScatter(place, part_ref, slots, stage, everything, rs_send, rs_recv, 0)
    scatter.start()
    summer = RowScatter(
        place, (grads_ref, pl.ds(0, half)), (grads_ref, pl.ds(half, half)), rows, *row_scratch
    )
    summer.start()
    scatter.forward()
    summer.second_start()
    scale = stats_ref[1:2, :]
    upstream = scatter.finish()
    scaled = (x_ref[...] - stats_ref[0:1, :]) * scale
    sums = begin_back(place, upstream, scaled, gain, stat, everything, sums_send, sums_recv, 0)
    vec_slots[place.row] = vec_ref[...]
    vec_slots[place.row, 10:11, 0:size] = token_sum(upstream * scaled)
    vec_slots[place.row, 11:12, 0:size] = token_sum(upstream)
    vec_copies = []
    for step in range(1, 8):
        peer = lax.rem(place.row + step, 8)
        copy = remote(
            vec_slots.at[place.row],
            vec_slots.at[place.row],
            vec_send.at[step - 1],
            vec_recv.at[step - 1],
            {"row": peer},
        )
        copy.start()
        vec_copies.append(copy)
    summer.third()
    gin_ref[...] = gx_ref[...] + end_back(sums, upstream, scaled, scale, gain, 4.0 * size)
    summer.fourth()
    summer.fifth()
    summer.finish(first_out, second_out)
    for copy in vec_copies:
        copy.wait()
    total = vec_slots[0]
    for index in range(1, 8):
        total = total + vec_slots[index]
    vecs_ref[...] = total


def communicate(kernel, number, shapes, scratch, *operands):
    return pl.pallas_call(
        kernel,
        out_shape=[jax.ShapeDtypeStruct(*shape) for shape in shapes],
        in_specs=[pl.BlockSpec(memory_space=pltpu.VMEM)] * len(operands),
        out_specs=[pl.BlockSpec(memory_space=pltpu.VMEM)] * len(shapes),
        scratch_shapes=scratch,
        compiler_params=pltpu.CompilerParams(
            collective_id=number, has_side_effects=True, vmem_limit_bytes=VMEM_LIMIT
        ),
    )(*operands)


def sems(*counts):
    pairs = []
    for count in counts:
        pairs += [pltpu.SemaphoreType.DMA((count,)), pltpu.SemaphoreType.DMA((count,))]
    return pairs


def allowed_pairs(keys, start, width, len_ref):
    key_pos = lax.broadcasted_iota(jnp.int32, (keys, 1), 0)
    query_pos = lax.broadcasted_iota(jnp.int32, (1, width), 1) + start
    key_seg, query_seg = jnp.zeros_like(key_pos), jnp.zeros_like(query_pos)
    end = 0
    for index in range(len_ref.shape[1]):
        end += len_ref[0, index]
        key_seg += jnp.where(key_pos >= end, 1, 0)
        query_seg += jnp.where(query_pos >= end, 1, 0)
    return (key_seg == query_seg) & (key_pos <= query_pos)


def attend_kernel(q_ref, k_ref, v_ref, len_ref, o_ref, log_ref):
    tokens = q_ref.shape[1]
    width = tokens // 4
    for start in range(0, tokens, width):
        keys = start + width
        mine = pl.ds(start, width)
        scores = left_product(k_ref[:, 0:keys], q_ref[:, mine])
        allowed = allowed_pairs(keys, start, width, len_ref)
        scores = jnp.where(allowed, scores, NEG)
        top = jnp.max(scores, axis=0, keepdims=True)
        expo = jnp.exp(scores - top)
        total = jnp.sum(expo, axis=0, keepdims=True)
        probs = (expo * (1.0 / total)).astype(jnp.bfloat16)
        o_ref[:, mine] = product(v_ref[:, 0:keys], probs).astype(o_ref.dtype)
        log_ref[0, :, mine] = top + jnp.log(total)


def attend_back_kernel(
    q_ref, k_ref, v_ref, go_ref, log_ref, len_ref,
    gq_ref, gk_ref, gv_ref, gk_sum, gv_sum,
):
    tokens = q_ref.shape[1]
    width = tokens // 4
    gk_sum[...] = jnp.zeros_like(gk_sum)
    gv_sum[...] = jnp.zeros_like(gv_sum)
    for start in range(0, tokens, width):
        keys = start + width
        mine = pl.ds(start, width)
        queries, upstream = q_ref[:, mine], go_ref[:, mine]
        scores = left_product(k_ref[:, 0:keys], queries)
        allowed = allowed_pairs(keys, start, width, len_ref)
        probs = jnp.exp(jnp.where(allowed, scores, NEG) - log_ref[0, :, mine])
        grad_probs = left_product(v_ref[:, 0:keys], upstream)
        inner = jnp.sum(probs * grad_probs, axis=0, keepdims=True)
        grad_scores = (probs * (grad_probs - inner)).astype(jnp.bfloat16)
        grad_q = product(k_ref[:, 0:keys], grad_scores).astype(jnp.bfloat16)
        gq_ref[:, mine] = (grad_q.astype(jnp.float32) * HEAD_DIM ** (-0.5)).astype(gq_ref.dtype)
        gk_sum[:, 0:keys] += right_product(queries, grad_scores)
        gv_sum[:, 0:keys] += right_product(upstream, probs.astype(jnp.bfloat16))
    gk_ref[...] = gk_sum[...].astype(gk_ref.dtype)
    gv_ref[...] = gv_sum[...].astype(gv_ref.dtype)


def head_spec(tokens, offset):
    return pl.BlockSpec((HEAD_DIM, tokens), lambda head: (head + offset, 0))


def len_spec():
    return pl.BlockSpec(memory_space=pltpu.SMEM)


def local_params():
    return pltpu.CompilerParams(vmem_limit_bytes=VMEM_LIMIT)


def attend(qkv, lengths):
    size, tokens = qkv.shape[0] // 3, qkv.shape[1]
    heads = size // HEAD_DIM
    log_spec = pl.BlockSpec((1, 1, tokens), lambda head: (head, 0, 0))
    return pl.pallas_call(
        attend_kernel,
        grid=(heads,),
        in_specs=[head_spec(tokens, part * heads) for part in range(3)]
        + [len_spec()],
        out_specs=[head_spec(tokens, 0), log_spec],
        out_shape=[
            jax.ShapeDtypeStruct((size, tokens), jnp.bfloat16),
            jax.ShapeDtypeStruct((heads, 1, tokens), jnp.float32),
        ],
        compiler_params=local_params(),
    )(qkv, qkv, qkv, lengths)


def attend_back(qkv, grad_mixed, log_total, lengths):
    size, tokens = qkv.shape[0] // 3, qkv.shape[1]
    heads = size // HEAD_DIM
    log_spec = pl.BlockSpec((1, 1, tokens), lambda head: (head, 0, 0))
    return pl.pallas_call(
        attend_back_kernel,
        grid=(heads,),
        in_specs=[head_spec(tokens, part * heads) for part in range(3)]
        + [head_spec(tokens, 0), log_spec, len_spec()],
        out_specs=[head_spec(tokens, 0)] * 3,
        out_shape=[jax.ShapeDtypeStruct((size, tokens), jnp.bfloat16)] * 3,
        scratch_shapes=[pltpu.VMEM((HEAD_DIM, tokens), jnp.float32)] * 2,
        compiler_params=local_params(),
    )(qkv, qkv, qkv, grad_mixed, log_total, lengths)


def fast_shards(
    layer_input,
    ln1_gain,
    ln1_bias,
    w_query,
    w_key,
    w_value,
    b_query,
    b_value,
    w_out,
    b_out,
    ln2_gain,
    ln2_bias,
    w_fc1,
    b_fc1,
    w_fc2,
    b_fc2,
    seq_lengths,
    cotangent,
):
    half, wide = jnp.bfloat16, jnp.float32
    size, tokens = layer_input.shape
    full = 4 * size
    rows, hidden_size = w_fc1.shape
    width = 4 * size + 2 * hidden_size
    scaling = HEAD_DIM ** (-0.5)
    params = jnp.stack([ln1_gain, ln1_bias, b_out, ln2_gain, ln2_bias, b_fc2], axis=1)
    stat = pltpu.VMEM((4, 8, tokens), wide)
    slots = pltpu.VMEM((3, size, tokens), half)
    stage = pltpu.VMEM((size, tokens), half)
    own_f32 = ((size, tokens), wide)
    all_half = ((full, tokens), half)
    stats_shape = ((8, tokens), wide)
    each = 3 * CHUNKS

    normed1, stats1, weights = communicate(
        enter_kernel,
        1,
        [all_half, stats_shape, ((full, full), half)],
        [stat] + sems(each, each) + row_gather_scratch(),
        layer_input,
        params,
        w_query,
        w_key,
        w_value,
        w_out.T,
    )
    w_qkv, w_up = weights[:, : 3 * size], weights[:, 3 * size :]
    qkv_bias = jnp.concatenate([b_query, jnp.zeros_like(b_query), b_value])[:, None]
    qkv_scale = jnp.where(jnp.arange(3 * size) < size, scaling, 1.0)[:, None]
    qkv = to_half((left_product(w_qkv, normed1) + qkv_bias) * qkv_scale)
    mixed, log_total = attend(qkv, seq_lengths)
    middle, normed2, grad_mlp, stats2, w_first, w_second = communicate(
        middle_kernel,
        2,
        [own_f32, all_half, all_half, stats_shape] + [((8 * rows, hidden_size), half)] * 2,
        [slots, stage, stat] + sems(each, each, each, 3) + row_gather_scratch(),
        to_half(product(w_up, mixed)),
        layer_input,
        cotangent,
        params,
        w_fc1,
        w_fc2.T,
    )
    hidden_pre = left_product(w_first, normed2) + b_fc1[:, None]
    activated, gate_pull = jax.vjp(smooth_gate, hidden_pre)
    hidden = to_half(activated)
    grad_pre = to_half(gate_pull(left_product(w_second, grad_mlp))[0])
    grad_middle, grad_branch, output, norm2_sums, sum_first, sum_second = communicate(
        turn_kernel,
        3,
        [own_f32, all_half, own_f32, ((8, size), wide)] + [((rows, hidden_size), wide)] * 2,
        [pltpu.VMEM((size, tokens), wide), slots, stage, slots, stage, stat]
        + sems(each, 3, each, each)
        + row_scatter_scratch(rows, hidden_size, half, wide),
        to_half(product(w_first, grad_pre)),
        to_half(product(w_second, hidden)),
        middle,
        cotangent,
        stats2,
        params,
        to_half(right_product(normed2, grad_pre)),
        to_half(right_product(grad_mlp, hidden)),
    )
    grad_mixed = to_half(left_product(w_up, grad_branch))
    grad_q, grad_k, grad_v = attend_back(qkv, grad_mixed, log_total, seq_lengths)
    grad_qkv = jnp.concatenate([grad_q, grad_k, grad_v], axis=0)
    grads = jnp.concatenate(
        [
            to_half(right_product(normed1, grad_qkv)),
            to_half(right_product(grad_branch, mixed)),
        ],
        axis=1,
    )

    def along(values):
        return jnp.sum(values.astype(wide), axis=1)

    vectors = jnp.concatenate(
        [
            along(grad_q)[None],
            along(grad_v)[None],
            along(to_half(grad_middle))[None],
            norm2_sums[0:2],
            along(to_half(cotangent))[None],
            along(grad_pre).reshape(hidden_size // size, size),
            jnp.zeros((6, size), wide),
        ],
        axis=0,
    )
    vectors = jnp.pad(vectors, ((0, 0), (0, 256 - size)))
    grad_input, sum_qk, sum_vo, vector_sums = communicate(
        leave_kernel,
        4,
        [own_f32] + [((rows, full // 2), wide)] * 2 + [(vectors.shape, wide)],
        [slots, stage, stat]
        + sems(3, 3)
        + [pltpu.VMEM((8,) + vectors.shape, wide)]
        + sems(7)
        + row_scatter_scratch(rows, full // 2, half, wide),
        to_half(product(w_qkv, grad_qkv)),
        layer_input,
        stats1,
        params,
        grad_middle,
        grads,
        vectors,
    )
    vector_sums = vector_sums[:, :size]
    return (
        output,
        grad_input,
        vector_sums[10],
        vector_sums[11],
        sum_qk[:, :size],
        sum_qk[:, size:],
        sum_vo[:, :size],
        vector_sums[0],
        vector_sums[1],
        sum_vo[:, size:].T,
        vector_sums[2],
        vector_sums[3],
        vector_sums[4],
        sum_first,
        vector_sums[6:10].reshape(-1),
        sum_second.T,
        vector_sums[5],
    )


def solution(mesh):
    in_specs = (
        P("col", "row"),
        P("col"),
        P("col"),
        P("row", "col"),
        P("row", "col"),
        P("row", "col"),
        P("col"),
        P("col"),
        P("col", "row"),
        P("col"),
        P("col"),
        P("col"),
        P("row", "col"),
        P("col"),
        P("col", "row"),
        P("col"),
        P("row", None),
        P("col", "row"),
    )
    out_specs = (
        P("col", "row"),
        P("col", "row"),
        P("col"),
        P("col"),
        P("row", "col"),
        P("row", "col"),
        P("row", "col"),
        P("col"),
        P("col"),
        P("col", "row"),
        P("col"),
        P("col"),
        P("col"),
        P("row", "col"),
        P("col"),
        P("col", "row"),
        P("col"),
    )
    fits = mesh.shape["col"] == 4 and mesh.shape["row"] == 8
    body = fast_shards if fits else shards
    return jax.shard_map(body, mesh=mesh, in_specs=in_specs, out_specs=out_specs, check_vma=False)
```

```python
import functools

import jax
import jax.numpy as jnp
from jax import lax
from jax.experimental import pallas as pl
from jax.experimental.pallas import tpu as pltpu
from jax.sharding import PartitionSpec as P

HEADS = 12
HEAD_DIM = 64


EPS = 1e-05
NEG = -1e30


def to_half(values):
    return values.astype(jnp.bfloat16)


def product(first_op, second_op):
    return jnp.dot(first_op, second_op, preferred_element_type=jnp.float32)


def product_left(first_op, second_op):
    return lax.dot_general(
        first_op, second_op, (((0,), (0,)), ((), ())), preferred_element_type=jnp.float32
    )


def product_right(first_op, second_op):
    return lax.dot_general(
        first_op, second_op, (((1,), (1,)), ((), ())), preferred_element_type=jnp.float32
    )


def column_sum(values):
    return jnp.sum(values.astype(jnp.float32), axis=0)


def smooth_gate(values):
    return jax.nn.gelu(values, approximate=True)


def query_positions(pack_rows):
    col_count = lax.axis_size("col")
    col_index = lax.axis_index("col")
    share_rows = pack_rows // col_count
    return col_index * share_rows + jnp.arange(share_rows, dtype=jnp.int32)


def feature_rows(block_rows):
    return lax.all_gather(block_rows, "col", axis=1, tiled=True)


def feature_sums(partial_value):
    return lax.psum_scatter(partial_value, "col", scatter_dimension=1, tiled=True)


def to_heads(block_rows):
    return lax.all_to_all(block_rows, "col", split_axis=0, concat_axis=1, tiled=True)


def to_features(block_rows):
    spread = lax.all_to_all(block_rows, "col", split_axis=1, concat_axis=0, tiled=True)
    return spread


def norm_forward(block_rows, norm_gain, norm_shift):
    local_width = block_rows.shape[1]
    full_width = local_width * lax.axis_size("col")
    row_sums, row_squares = lax.psum(
        (jnp.sum(block_rows, axis=1), jnp.sum(block_rows * block_rows, axis=1)), "col"
    )
    row_mean = (row_sums / full_width)[:, None]
    variance = (row_squares / full_width)[:, None] - row_mean * row_mean
    row_scale = lax.rsqrt(variance + EPS)
    scaled = (block_rows - row_mean) * row_scale
    normed = feature_rows(to_half(scaled * norm_gain + norm_shift))
    return (normed, scaled, row_scale)


def norm_backward(upstream, scaled, row_scale, norm_gain):
    full_width = upstream.shape[1] * lax.axis_size("col")
    weighted = upstream * norm_gain
    row_sums, row_along = lax.psum(
        (jnp.sum(weighted, axis=1), jnp.sum(weighted * scaled, axis=1)), "col"
    )
    grad_rows = row_scale * (
        weighted - (row_sums / full_width)[:, None] - scaled * (row_along / full_width)[:, None]
    )
    return (grad_rows, jnp.sum(upstream * scaled, axis=0), jnp.sum(upstream, axis=0))


def split_heads(block_rows):
    return block_rows.reshape(block_rows.shape[0], HEADS, HEAD_DIM)


def masked_scores(queries, all_keys, query_pos, segment):
    scores = jnp.einsum(
        "qhd,khd->hqk",
        split_heads(queries),
        split_heads(all_keys),
        preferred_element_type=jnp.float32,
    )
    key_pos = jnp.arange(all_keys.shape[0], dtype=jnp.int32)
    allowed = (segment[query_pos][:, None] == segment[None, :]) & (
        key_pos[None, :] <= query_pos[:, None]
    )
    return jnp.where(allowed[None], scores, NEG)


def attention_forward(queries, all_keys, all_values, query_pos, segment):
    scores = masked_scores(queries, all_keys, query_pos, segment)
    row_top = jnp.max(scores, axis=2, keepdims=True)
    expo_vals = jnp.exp(scores - row_top)
    row_total = jnp.sum(expo_vals, axis=2, keepdims=True)
    attn_probs = to_half(expo_vals / row_total)
    mixed = jnp.einsum(
        "hqk,khd->qhd", attn_probs, split_heads(all_values), preferred_element_type=jnp.float32
    )
    return (mixed.reshape(queries.shape[0], -1), row_top + jnp.log(row_total))


def attention_backward(queries, all_keys, all_values, query_pos, segment, log_total, grad_mixed):
    scores = masked_scores(queries, all_keys, query_pos, segment)
    attn_probs = jnp.exp(scores - log_total)
    grad_heads = split_heads(grad_mixed)
    grad_probs = jnp.einsum(
        "qhd,khd->hqk", grad_heads, split_heads(all_values), preferred_element_type=jnp.float32
    )
    row_inner = jnp.sum(attn_probs * grad_probs, axis=2, keepdims=True)
    grad_scores = to_half(attn_probs * (grad_probs - row_inner))
    grad_queries = jnp.einsum(
        "hqk,khd->qhd", grad_scores, split_heads(all_keys), preferred_element_type=jnp.float32
    )
    grad_keys = jnp.einsum(
        "hqk,qhd->khd", grad_scores, split_heads(queries), preferred_element_type=jnp.float32
    )
    grad_values = jnp.einsum(
        "hqk,qhd->khd", to_half(attn_probs), grad_heads, preferred_element_type=jnp.float32
    )
    key_count = all_keys.shape[0]
    return (
        grad_queries.reshape(queries.shape[0], -1),
        grad_keys.reshape(key_count, -1),
        grad_values.reshape(key_count, -1),
    )


def shards(
    layer_input,
    ln1_gain,
    ln1_bias,
    w_query,
    w_key,
    w_value,
    b_query,
    b_value,
    w_out,
    b_out,
    ln2_gain,
    ln2_bias,
    w_fc1,
    b_fc1,
    w_fc2,
    b_fc2,
    seq_lengths,
    cotangent,
):
    scaling = HEAD_DIM ** (-0.5)
    input_rows = layer_input.T
    cotangent_rows = cotangent.T
    pack_rows = input_rows.shape[0]
    seq_ends = jnp.cumsum(seq_lengths[0])
    places = jnp.arange(pack_rows, dtype=jnp.int32)
    segment = jnp.sum((places[:, None] >= seq_ends[None, :]).astype(jnp.int32), axis=1)
    query_pos = query_positions(pack_rows)
    gathered = (
        lax.all_gather(w_query, "row", axis=0, tiled=True),
        lax.all_gather(w_key, "row", axis=0, tiled=True),
        lax.all_gather(w_value, "row", axis=0, tiled=True),
        lax.all_gather(w_fc1, "row", axis=0, tiled=True),
        lax.all_gather(w_out.T, "row", axis=0, tiled=True),
        lax.all_gather(w_fc2.T, "row", axis=0, tiled=True),
    )
    full_query, full_key, full_value, full_fc1, full_out, full_fc2 = gathered
    normed1, scaled1, scale1 = norm_forward(input_rows, ln1_gain, ln1_bias)
    query_part = to_half((product(normed1, full_query) + b_query) * scaling)
    key_part = to_half(product(normed1, full_key))
    value_part = to_half(product(normed1, full_value) + b_value)
    queries = to_heads(query_part)
    all_keys, all_values = (
        lax.all_gather(key_part, "col", axis=1, tiled=True),
        lax.all_gather(value_part, "col", axis=1, tiled=True),
    )
    attended, log_total = attention_forward(queries, all_keys, all_values, query_pos, segment)
    spread = to_features(to_half(attended))
    middle = input_rows + feature_sums(product_right(spread, full_out)) + b_out
    normed2, scaled2, scale2 = norm_forward(middle, ln2_gain, ln2_bias)
    hidden_pre = product(normed2, full_fc1) + b_fc1
    activated, gate_pull = jax.vjp(smooth_gate, hidden_pre)
    hidden = to_half(activated)
    output = middle + feature_sums(product_right(hidden, full_fc2)) + b_fc2
    grad_mlp = to_half(cotangent_rows)
    grad_mlp_full = feature_rows(grad_mlp)
    grad_hidden = product(grad_mlp_full, full_fc2)
    grad_pre = to_half(gate_pull(grad_hidden)[0])
    grad_fc2_t = product_left(grad_mlp_full, hidden)
    grad_fc1 = product_left(normed2, grad_pre)
    grad_normed2 = feature_sums(product_right(grad_pre, full_fc1))
    back_second, gain2_grad, shift2_grad = norm_backward(grad_normed2, scaled2, scale2, ln2_gain)
    grad_middle = cotangent_rows + back_second
    grad_branch = to_half(grad_middle)
    grad_branch_full = feature_rows(grad_branch)
    grad_out_t = product_left(grad_branch_full, spread)
    grad_spread = to_half(product(grad_branch_full, full_out))
    grad_attended = to_heads(grad_spread)
    grad_q_heads, grad_k_part, grad_v_part = attention_backward(
        queries, all_keys, all_values, query_pos, segment, log_total, grad_attended
    )
    grad_query_raw = to_features(to_half(grad_q_heads)).astype(jnp.float32) * scaling
    grad_query = to_half(grad_query_raw)
    key_total, value_total = (
        lax.psum_scatter(
            grad_k_part.astype(jnp.bfloat16), "col", scatter_dimension=1, tiled=True
        ).astype(jnp.float32),
        lax.psum_scatter(
            grad_v_part.astype(jnp.bfloat16), "col", scatter_dimension=1, tiled=True
        ).astype(jnp.float32),
    )
    grad_key = to_half(key_total)
    grad_value = to_half(value_total)
    grad_normed1 = feature_sums(
        product_right(grad_query, full_query)
        + product_right(grad_key, full_key)
        + product_right(grad_value, full_value)
    )
    back_first, gain1_grad, shift1_grad = norm_backward(grad_normed1, scaled1, scale1, ln1_gain)
    grad_input = grad_middle + back_first
    weight_sums = (
        lax.psum_scatter(
            product_left(normed1, grad_query).astype(jnp.bfloat16),
            "row",
            scatter_dimension=0,
            tiled=True,
        ).astype(jnp.float32),
        lax.psum_scatter(
            product_left(normed1, grad_key).astype(jnp.bfloat16),
            "row",
            scatter_dimension=0,
            tiled=True,
        ).astype(jnp.float32),
        lax.psum_scatter(
            product_left(normed1, grad_value).astype(jnp.bfloat16),
            "row",
            scatter_dimension=0,
            tiled=True,
        ).astype(jnp.float32),
        lax.psum_scatter(
            grad_out_t.astype(jnp.bfloat16), "row", scatter_dimension=0, tiled=True
        ).astype(jnp.float32),
        lax.psum_scatter(
            grad_fc1.astype(jnp.bfloat16), "row", scatter_dimension=0, tiled=True
        ).astype(jnp.float32),
        lax.psum_scatter(
            grad_fc2_t.astype(jnp.bfloat16), "row", scatter_dimension=0, tiled=True
        ).astype(jnp.float32),
    )
    vector_sums = lax.psum(
        (
            gain1_grad,
            shift1_grad,
            column_sum(grad_query_raw),
            column_sum(grad_value),
            column_sum(grad_branch),
            gain2_grad,
            shift2_grad,
            column_sum(grad_pre),
            column_sum(grad_mlp),
        ),
        "row",
    )
    return (
        output.T,
        grad_input.T,
        vector_sums[0],
        vector_sums[1],
        weight_sums[0],
        weight_sums[1],
        weight_sums[2],
        vector_sums[2],
        vector_sums[3],
        weight_sums[3].T,
        vector_sums[4],
        vector_sums[5],
        vector_sums[6],
        weight_sums[4],
        vector_sums[7],
        weight_sums[5].T,
        vector_sums[8],
    )


VMEM_LIMIT = 56 * 1024 * 1024
MESH_IDS = pl.DeviceIdType.MESH


def left_product(first_op, second_op, **extra):
    return lax.dot_general(
        first_op, second_op, (((0,), (0,)), ((), ())), preferred_element_type=jnp.float32, **extra
    )


def right_product(first_op, second_op, **extra):
    return lax.dot_general(
        first_op, second_op, (((1,), (1,)), ((), ())), preferred_element_type=jnp.float32, **extra
    )


def remote(source, target, send_sem, recv_sem, device):
    return pltpu.make_async_remote_copy(
        src_ref=source,
        dst_ref=target,
        send_sem=send_sem,
        recv_sem=recv_sem,
        device_id=device,
        device_id_type=MESH_IDS,
    )


class Place:
    def __init__(self):
        self.col = lax.axis_index("col")
        self.row = lax.axis_index("row")
        self.core_peer = self.col + 1 - 2 * lax.rem(self.col, 2)
        self.chip_peer = lax.rem(self.col + 2, 4)
        self.far_peer = lax.rem(self.core_peer + 2, 4)
        self.z = self.row // 2
        self.y = lax.rem(self.row, 2)
        self.y_peer = self.row + 1 - 2 * self.y


def greet(place, rows_too):
    barrier = pltpu.get_barrier_semaphore()
    count = 3
    for step in range(1, 4):
        peer = lax.rem(place.col + step, 4)
        pl.semaphore_signal(barrier, inc=1, device_id={"col": peer}, device_id_type=MESH_IDS)
    if rows_too:
        count += 7
        for step in range(1, 8):
            peer = lax.rem(place.row + step, 8)
            pl.semaphore_signal(barrier, inc=1, device_id={"row": peer}, device_id_type=MESH_IDS)
    pl.semaphore_wait(barrier, count)


class ColGather:
    def __init__(self, place, buf, columns, send, recv, base):
        self.place, self.buf, self.columns = place, buf, columns
        self.send, self.recv, self.base = send, recv, base
        self.size = buf.shape[0] // 4

    def block(self, index):
        rows = pl.ds(pl.multiple_of(index * self.size, self.size), self.size)
        return self.buf.at[rows, self.columns]

    def move(self, slot, source, device):
        slot += self.base
        return remote(source, source, self.send.at[slot], self.recv.at[slot], {"col": device})

    def start(self):
        own = self.block(self.place.col)
        self.chip = self.move(0, own, self.place.chip_peer)
        self.core = self.move(1, own, self.place.core_peer)
        self.chip.start()
        self.core.start()

    def forward(self):
        self.chip.wait_recv()
        got = self.block(self.place.chip_peer)
        self.onward = self.move(2, got, self.place.core_peer)
        self.onward.start()

    def finish(self):
        self.chip.wait_send()
        self.core.wait()
        self.onward.wait()


class ColScatter:
    def __init__(self, place, part, slots, stage, columns, send, recv, base):
        self.place, self.part, self.columns = place, part, columns
        self.slots, self.stage = slots, stage
        self.send, self.recv, self.base = send, recv, base
        self.size = part.shape[0] // 4

    def block(self, index):
        rows = pl.ds(pl.multiple_of(index * self.size, self.size), self.size)
        return self.part.at[rows, self.columns]

    def slot(self, index):
        return self.slots.at[index, :, self.columns]

    def move(self, slot, source, device):
        sem = slot + self.base
        return remote(
            source, self.slot(slot), self.send.at[sem], self.recv.at[sem], {"col": device}
        )

    def start(self):
        place = self.place
        self.far = self.move(0, self.block(place.far_peer), place.core_peer)
        self.far.start()
        self.near = self.move(1, self.block(place.core_peer), place.core_peer)
        self.near.start()

    def forward(self):
        self.far.wait_recv()
        mixed = self.block(self.place.chip_peer)[...].astype(jnp.float32) + self.slot(0)[
            ...
        ].astype(jnp.float32)
        staged = self.stage.at[:, self.columns]
        staged[...] = mixed.astype(self.stage.dtype)
        self.cross = self.move(2, staged, self.place.chip_peer)
        self.cross.start()

    def finish(self):
        self.far.wait_send()
        self.near.wait()
        self.cross.wait()
        own = self.block(self.place.col)[...].astype(jnp.float32)
        return own + self.slot(1)[...].astype(jnp.float32) + self.slot(2)[...].astype(jnp.float32)


class ColSums:
    def __init__(self, place, first, second, stat, columns, send, recv, base):
        self.stat, self.columns = stat, columns
        stat[place.col, 0:1, columns] = first
        stat[place.col, 1:2, columns] = second
        own = stat.at[place.col, :, columns]
        self.copies = []
        for step in range(1, 4):
            peer = lax.rem(place.col + step, 4)
            sem = base + step - 1
            copy = remote(own, own, send.at[sem], recv.at[sem], {"col": peer})
            copy.start()
            self.copies.append(copy)

    def finish(self):
        for copy in self.copies:
            copy.wait()
        part = [self.stat[index, :, self.columns] for index in range(4)]
        total = part[0] + part[1] + part[2] + part[3]
        return total[0:1], total[1:2]


def begin_stats(place, values, *rest):
    return ColSums(
        place,
        jnp.sum(values, axis=0, keepdims=True),
        jnp.sum(values * values, axis=0, keepdims=True),
        *rest,
    )


def end_stats(sums, width):
    total, squares = sums.finish()
    mean = total / width
    return mean, lax.rsqrt(squares / width - mean * mean + EPS)


def begin_back(place, upstream, scaled, gain, *rest):
    weighted = upstream * gain
    return ColSums(
        place,
        jnp.sum(weighted, axis=0, keepdims=True),
        jnp.sum(weighted * scaled, axis=0, keepdims=True),
        *rest,
    )


def end_back(sums, upstream, scaled, scale, gain, width):
    total, along = sums.finish()
    return scale * (upstream * gain - total / width - scaled * (along / width))


def token_sum(values):
    ones = jnp.ones((8, values.shape[1]), jnp.float32)
    return right_product(ones, values, precision=lax.Precision.HIGHEST)[0:1]


class LineGather:
    def __init__(self, place, buf, columns, size, stride, offset, send, recv, onward=None):
        self.place, self.buf, self.columns, self.size = place, buf, columns, size
        self.stride, self.offset, self.send, self.recv = stride, offset, send, recv
        self.onward = onward

    def copy(self, hop, way):
        source = self.place.z - way * hop
        start = pl.multiple_of(jnp.clip(source, 0, 3) * self.stride + self.offset, 16)
        block = self.buf.at[pl.ds(start, self.size), self.columns]
        slot = 4 * (1 if way < 0 else 0)
        target = jnp.clip(self.place.row + 2 * way, 0, 7)
        return remote(
            block, block, self.send.at[slot + hop], self.recv.at[slot + hop + 1], {"row": target}
        )

    def arrived(self, hop, way):
        slot = 4 * (1 if way < 0 else 0)
        start = pl.multiple_of(
            jnp.clip(self.place.z - way * hop, 0, 3) * self.stride + self.offset, 16
        )
        block = self.buf.at[pl.ds(start, self.size), self.columns]
        pltpu.make_async_copy(block, block, self.recv.at[slot + hop]).wait()

    def has(self, hop, way):
        return self.place.z >= hop if way > 0 else self.place.z + hop <= 3

    def sends(self, hop, way):
        more = self.place.z < 3 if way > 0 else self.place.z > 0
        return jnp.logical_and(self.has(hop, way), more)

    def start(self):
        for way in (1, -1):

            @pl.when(self.sends(0, way))
            def _():
                self.copy(0, way).start()

    def step(self, hop):
        for way in (1, -1):

            @pl.when(self.has(hop, way))
            def _():
                self.arrived(hop, way)
                if self.onward is not None:
                    self.onward(hop, way).start()

            if hop < 3:

                @pl.when(self.sends(hop, way))
                def _():
                    self.copy(hop, way).start()

    def finish(self):
        if self.onward is not None:
            for hop in range(1, 4):
                for way in (1, -1):

                    @pl.when(self.has(hop, way))
                    def _():
                        self.onward(hop, way).wait()

        for hop in range(3):
            for way in (1, -1):

                @pl.when(self.sends(hop, way))
                def _():
                    self.copy(hop, way).wait_send()


class LineScatter:
    def __init__(self, place, block, right, left, send, recv):
        self.place, self.block, self.right, self.left = place, block, right, left
        self.send, self.recv = send, recv

    def copy(self, target_z, way):
        slots = self.right if way > 0 else self.left
        base = 0 if way > 0 else 4
        device = {"row": jnp.clip(self.place.row + 2 * way, 0, 7)}
        return remote(
            slots.at[target_z],
            slots.at[target_z],
            self.send.at[base + target_z],
            self.recv.at[base + target_z],
            device,
        )

    def step(self, index):
        z = self.place.z
        for way, target_z in ((1, 3 - index), (-1, index)):
            slots = self.right if way > 0 else self.left
            relays = z < target_z if way > 0 else z > target_z
            edge = z == 0 if way > 0 else z == 3
            inner = z > 0 if way > 0 else z < 3

            @pl.when(jnp.logical_and(relays, edge))
            def _():
                slots[target_z] = self.block(target_z)[...]

            @pl.when(jnp.logical_and(relays, inner))
            def _():
                self.copy(target_z, way).wait_recv()
                mixed = slots[target_z].astype(jnp.float32) + self.block(target_z)[...].astype(
                    jnp.float32
                )
                slots[target_z] = mixed.astype(slots.dtype)

            @pl.when(relays)
            def _():
                self.copy(target_z, way).start()

    def finish(self, total):
        z = self.place.z
        for target_z in range(4):

            @pl.when(z == target_z)
            def _():
                total[...] = self.block(target_z)[...].astype(jnp.float32)
                if target_z > 0:
                    self.copy(target_z, 1).wait_recv()
                    total[...] += self.right[target_z].astype(jnp.float32)
                if target_z < 3:
                    self.copy(target_z, -1).wait_recv()
                    total[...] += self.left[target_z].astype(jnp.float32)

            if target_z > 0:

                @pl.when(z < target_z)
                def _():
                    self.copy(target_z, 1).wait_send()

            if target_z < 3:

                @pl.when(z > target_z)
                def _():
                    self.copy(target_z, -1).wait_send()


def row_gather_scratch():
    return sems(8, 8, 8)


class RowGather:
    def __init__(self, place, first, second, rows, send_a, recv_a, send_b, recv_b, y_send, y_recv):
        self.place, self.rows = place, rows
        self.first, self.first_columns = first
        self.second, self.second_columns = second
        self.y_send, self.y_recv = y_send, y_recv
        self.line_a = LineGather(
            place, self.first, self.first_columns, rows, 2 * rows, place.y * rows,
            send_a, recv_a, self.onward,
        )
        self.line_b = LineGather(
            place, self.second, self.second_columns, 2 * rows, 2 * rows, 0, send_b, recv_b
        )

    def across(self, buf, columns, source_z, slot):
        start = pl.multiple_of(source_z * 2 * self.rows + self.place.y * self.rows, self.rows)
        block = buf.at[pl.ds(start, self.rows), columns]
        peer = {"row": self.place.y_peer}
        return remote(block, block, self.y_send.at[slot], self.y_recv.at[slot], peer)

    def onward(self, hop, way):
        source = jnp.clip(self.place.z - way * hop, 0, 3)
        slot = hop if way > 0 else hop + 3
        return self.across(self.first, self.first_columns, source, slot)

    def start(self):
        self.pair = self.across(self.second, self.second_columns, self.place.z, 7)
        self.pair.start()
        self.line_a.start()

    def second_start(self):
        self.pair.wait()
        self.line_b.start()
        self.mine = self.onward(0, 1)
        self.mine.start()

    def step(self, hop):
        self.line_a.step(hop)
        self.line_b.step(hop)

    def finish(self):
        self.mine.wait()
        self.line_a.finish()
        self.line_b.finish()


def row_scatter_scratch(rows, columns, half, wide):
    return (
        [pltpu.VMEM((4, rows, columns), half)] * 3
        + [pltpu.VMEM((4, 2 * rows, columns), half)] * 2
        + [
            pltpu.VMEM((2 * rows, columns), wide),
            pltpu.VMEM((rows, columns), half),
            pltpu.VMEM((rows, columns), half),
        ]
        + sems(5, 8, 8)
    )


class RowScatter:
    def __init__(
        self, place, first, second, rows, slots, right_a, left_a, right_b, left_b,
        total, stage, last, y_send, y_recv, send_a, recv_a, send_b, recv_b,
    ):
        self.place, self.rows, self.slots = place, rows, slots
        self.first, self.first_columns = first
        self.second, self.second_columns = second
        self.total, self.stage, self.last = total, stage, last
        self.y_send, self.y_recv = y_send, y_recv
        self.line_a = LineScatter(place, lambda k: slots.at[k], right_a, left_a, send_a, recv_a)
        self.line_b = LineScatter(
            place,
            lambda k: self.second.at[pl.ds(k * 2 * rows, 2 * rows), self.second_columns],
            right_b, left_b, send_b, recv_b,
        )

    def block(self, target_z, target_y):
        start = pl.multiple_of(target_z * 2 * self.rows + target_y * self.rows, self.rows)
        return self.first.at[pl.ds(start, self.rows), self.first_columns]

    def start(self):
        self.copies = {}
        for target_z in (3, 0, 2, 1):
            self.copies[target_z] = remote(
                self.block(target_z, 1 - self.place.y),
                self.slots.at[target_z],
                self.y_send.at[target_z],
                self.y_recv.at[target_z],
                {"row": self.place.y_peer},
            )
            self.copies[target_z].start()
        self.line_b.step(0)

    def mix(self, target_z):
        self.copies[target_z].wait()
        mixed = self.slots[target_z].astype(jnp.float32) + self.block(target_z, self.place.y)[
            ...
        ].astype(jnp.float32)
        self.slots[target_z] = mixed.astype(self.slots.dtype)

    def second_start(self):
        self.mix(3)
        self.mix(0)
        self.line_a.step(0)
        self.mix(2)
        self.mix(1)

    def third(self):
        self.line_b.step(1)
        self.line_a.step(1)

    def fourth(self):
        self.line_b.step(2)
        self.line_a.step(2)

    def fifth(self):
        rows = self.rows
        self.line_b.finish(self.total)
        theirs = pl.ds(pl.multiple_of((1 - self.place.y) * rows, rows), rows)
        self.stage[...] = self.total[theirs, :].astype(self.stage.dtype)
        self.final = remote(
            self.stage, self.last, self.y_send.at[4], self.y_recv.at[4], {"row": self.place.y_peer}
        )
        self.final.start()

    def finish(self, first_out, second_out):
        rows = self.rows
        self.line_a.finish(first_out)
        self.final.wait()
        ours = pl.ds(pl.multiple_of(self.place.y * rows, rows), rows)
        second_out[...] = self.total[ours, :] + self.last[...].astype(jnp.float32)


CHUNKS = 2


def chunks_of(tokens):
    width = tokens // CHUNKS
    return [pl.ds(index * width, width) for index in range(CHUNKS)]


GAIN1, SHIFT1, BIAS_OUT, GAIN2, SHIFT2, BIAS_FC2 = range(6)


def enter_kernel(
    x_ref, par_ref, wq_ref, wk_ref, wv_ref, wo_ref,
    h_ref, stats_ref, full_ref,
    stat, sums_send, sums_recv, h_send, h_recv, *row_scratch,
):
    place = Place()
    greet(place, True)
    size = x_ref.shape[0]
    rows = wq_ref.shape[0]
    half = 2 * size
    chunks = chunks_of(x_ref.shape[1])
    own = pl.ds(pl.multiple_of(place.col * size, size), size)
    own_rows = pl.ds(pl.multiple_of(place.row * rows, rows), rows)
    for index, ref in enumerate((wq_ref, wk_ref, wv_ref, wo_ref)):
        full_ref[own_rows, index * size : (index + 1) * size] = ref[...]
    gather = RowGather(
        place, (full_ref, pl.ds(0, half)), (full_ref, pl.ds(half, half)), rows, *row_scratch
    )
    gather.start()
    sums = [
        begin_stats(place, x_ref[:, cols], stat, cols, sums_send, sums_recv, 3 * index)
        for index, cols in enumerate(chunks)
    ]
    gathers = []
    for index, cols in enumerate(chunks):
        mean, scale = end_stats(sums[index], 4.0 * size)
        stats_ref[0:1, cols] = mean
        stats_ref[1:2, cols] = scale
        normed = (x_ref[:, cols] - mean) * scale * par_ref[:, GAIN1 : GAIN1 + 1]
        h_ref[own, cols] = (normed + par_ref[:, SHIFT1 : SHIFT1 + 1]).astype(h_ref.dtype)
        gathers.append(ColGather(place, h_ref, cols, h_send, h_recv, 3 * index))
        gathers[-1].start()
    gather.second_start()
    gather.step(1)
    gathers[0].forward()
    gather.step(2)
    gathers[1].forward()
    gather.step(3)
    for item in gathers:
        item.finish()
    gather.finish()


def middle_kernel(
    part_ref, x_ref, cot_ref, par_ref, first_ref, second_ref,
    mid_ref, h_ref, gm_ref, stats_ref, full_first, full_second,
    slots, stage, stat, rs_send, rs_recv, sums_send, sums_recv, h_send, h_recv,
    gm_send, gm_recv, *row_scratch,
):
    place = Place()
    greet(place, True)
    size = x_ref.shape[0]
    rows, columns = first_ref.shape
    chunks = chunks_of(x_ref.shape[1])
    own = pl.ds(pl.multiple_of(place.col * size, size), size)
    scatters = [
        ColScatter(place, part_ref, slots, stage, cols, rs_send, rs_recv, 3 * index)
        for index, cols in enumerate(chunks)
    ]
    for item in scatters:
        item.start()
    own_rows = pl.ds(pl.multiple_of(place.row * rows, rows), rows)
    full_first[own_rows, :] = first_ref[...]
    full_second[own_rows, :] = second_ref[...]
    everything = pl.ds(0, columns)
    gather = RowGather(
        place, (full_first, everything), (full_second, everything), rows, *row_scratch
    )
    gather.start()
    for item in scatters:
        item.forward()
    gm_ref[own, :] = cot_ref[...].astype(gm_ref.dtype)
    gather.second_start()
    sums, gathers = [], []

    def begin(index):
        cols = chunks[index]
        values = scatters[index].finish() + x_ref[:, cols] + par_ref[:, BIAS_OUT : BIAS_OUT + 1]
        mid_ref[:, cols] = values
        sums.append(begin_stats(place, values, stat, cols, sums_send, sums_recv, 3 * index))

    def end(index):
        cols = chunks[index]
        mean, scale = end_stats(sums[index], 4.0 * size)
        stats_ref[0:1, cols] = mean
        stats_ref[1:2, cols] = scale
        normed = (mid_ref[:, cols] - mean) * scale * par_ref[:, GAIN2 : GAIN2 + 1]
        h_ref[own, cols] = (normed + par_ref[:, SHIFT2 : SHIFT2 + 1]).astype(h_ref.dtype)
        gathers.append(ColGather(place, h_ref, cols, h_send, h_recv, 3 * index))
        gathers[-1].start()

    gather.line_a.step(1)
    begin(0)
    begin(1)
    gather.line_b.step(1)
    end(0)
    gather.line_a.step(2)
    end(1)
    everywhere = pl.ds(0, x_ref.shape[1])
    gathers.append(ColGather(place, gm_ref, everywhere, gm_send, gm_recv, 0))
    gathers[2].start()
    gather.line_b.step(2)
    gathers[0].forward()
    gathers[1].forward()
    gather.step(3)
    gathers[2].forward()
    for item in gathers:
        item.finish()
    gather.finish()


def turn_kernel(
    part_ref, out_part_ref, mid_ref, cot_ref, stats_ref, par_ref, first_ref, second_ref,
    gx_ref, ga_ref, out_ref, vec_ref, first_out, second_out,
    up_keep, slots, stage, out_slots, out_stage, stat, rs_send, rs_recv, out_send, out_recv, sums_send, sums_recv, ga_send, ga_recv,
    *row_scratch,
):
    place = Place()
    greet(place, True)
    size = mid_ref.shape[0]
    rows = first_out.shape[0]
    everything = pl.ds(0, first_ref.shape[1])
    chunks = chunks_of(mid_ref.shape[1])
    own = pl.ds(pl.multiple_of(place.col * size, size), size)
    gain = par_ref[:, GAIN2 : GAIN2 + 1]
    scatters = [
        ColScatter(place, part_ref, slots, stage, cols, rs_send, rs_recv, 3 * index)
        for index, cols in enumerate(chunks)
    ]
    for item in scatters:
        item.start()
    summer = RowScatter(
        place, (first_ref, everything), (second_ref, everything), rows, *row_scratch
    )
    summer.start()
    out_scatter = ColScatter(
        place, out_part_ref, out_slots, out_stage, pl.ds(0, mid_ref.shape[1]), out_send, out_recv, 0
    )
    out_scatter.start()
    for item in scatters:
        item.forward()
    summer.second_start()
    sums, gathers = [], []

    def scaled(cols):
        return (mid_ref[:, cols] - stats_ref[0:1, cols]) * stats_ref[1:2, cols]

    def begin(index):
        cols = chunks[index]
        upstream = scatters[index].finish()
        up_keep[:, cols] = upstream
        xhat = scaled(cols)
        sums.append(
            begin_back(place, upstream, xhat, gain, stat, cols, sums_send, sums_recv, 3 * index)
        )

    def end(index):
        cols = chunks[index]
        back = end_back(
            sums[index], up_keep[:, cols], scaled(cols), stats_ref[1:2, cols], gain, 4.0 * size
        )
        gx = cot_ref[:, cols] + back
        gx_ref[:, cols] = gx
        ga_ref[own, cols] = gx.astype(ga_ref.dtype)
        gathers.append(ColGather(place, ga_ref, cols, ga_send, ga_recv, 3 * index))
        gathers[-1].start()

    summer.third()
    begin(0)
    begin(1)
    end(0)
    end(1)
    summer.fourth()
    out_scatter.forward()
    gathers[0].forward()
    gathers[1].forward()
    summer.fifth()
    vec_ref[0:1, :] = token_sum(up_keep[...] * scaled(pl.ds(0, mid_ref.shape[1])))
    vec_ref[1:2, :] = token_sum(up_keep[...])
    for item in gathers:
        item.finish()
    out_ref[...] = out_scatter.finish() + mid_ref[...] + par_ref[:, BIAS_FC2 : BIAS_FC2 + 1]
    summer.finish(first_out, second_out)


def leave_kernel(
    part_ref, x_ref, stats_ref, par_ref, gx_ref, grads_ref, vec_ref,
    gin_ref, first_out, second_out, vecs_ref,
    slots, stage, stat, rs_send, rs_recv, sums_send, sums_recv,
    vec_slots, vec_send, vec_recv, *row_scratch,
):
    place = Place()
    greet(place, True)
    size = x_ref.shape[0]
    rows = first_out.shape[0]
    half = grads_ref.shape[1] // 2
    everything = pl.ds(0, x_ref.shape[1])
    gain = par_ref[:, GAIN1 : GAIN1 + 1]
    scatter = ColScatter(place, part_ref, slots, stage, everything, rs_send, rs_recv, 0)
    scatter.start()
    summer = RowScatter(
        place, (grads_ref, pl.ds(0, half)), (grads_ref, pl.ds(half, half)), rows, *row_scratch
    )
    summer.start()
    summer.second_start()
    scatter.forward()
    summer.third()
    scale = stats_ref[1:2, :]
    upstream = scatter.finish()
    scaled = (x_ref[...] - stats_ref[0:1, :]) * scale
    sums = begin_back(place, upstream, scaled, gain, stat, everything, sums_send, sums_recv, 0)
    vec_slots[place.row] = vec_ref[...]
    vec_slots[place.row, 10:11, 0:size] = token_sum(upstream * scaled)
    vec_slots[place.row, 11:12, 0:size] = token_sum(upstream)
    vec_copies = []
    for step in range(1, 8):
        peer = lax.rem(place.row + step, 8)
        copy = remote(
            vec_slots.at[place.row],
            vec_slots.at[place.row],
            vec_send.at[step - 1],
            vec_recv.at[step - 1],
            {"row": peer},
        )
        copy.start()
        vec_copies.append(copy)
    summer.fourth()
    gin_ref[...] = gx_ref[...] + end_back(sums, upstream, scaled, scale, gain, 4.0 * size)
    summer.fifth()
    summer.finish(first_out, second_out)
    for copy in vec_copies:
        copy.wait()
    total = vec_slots[0]
    for index in range(1, 8):
        total = total + vec_slots[index]
    vecs_ref[...] = total


def communicate(kernel, number, shapes, scratch, *operands):
    return pl.pallas_call(
        kernel,
        out_shape=[jax.ShapeDtypeStruct(*shape) for shape in shapes],
        in_specs=[pl.BlockSpec(memory_space=pltpu.VMEM)] * len(operands),
        out_specs=[pl.BlockSpec(memory_space=pltpu.VMEM)] * len(shapes),
        scratch_shapes=scratch,
        compiler_params=pltpu.CompilerParams(
            collective_id=number, has_side_effects=True, vmem_limit_bytes=VMEM_LIMIT
        ),
    )(*operands)


def sems(*counts):
    pairs = []
    for count in counts:
        pairs += [pltpu.SemaphoreType.DMA((count,)), pltpu.SemaphoreType.DMA((count,))]
    return pairs


def allowed_pairs(keys, start, width, len_ref):
    key_pos = lax.broadcasted_iota(jnp.int32, (keys, 1), 0)
    query_pos = lax.broadcasted_iota(jnp.int32, (1, width), 1) + start
    key_seg, query_seg = jnp.zeros_like(key_pos), jnp.zeros_like(query_pos)
    end = 0
    for index in range(len_ref.shape[1]):
        end += len_ref[0, index]
        key_seg += jnp.where(key_pos >= end, 1, 0)
        query_seg += jnp.where(query_pos >= end, 1, 0)
    return (key_seg == query_seg) & (key_pos <= query_pos)


def attend_kernel(q_ref, k_ref, v_ref, len_ref, o_ref, log_ref):
    tokens = q_ref.shape[1]
    width = tokens // 4
    for start in range(0, tokens, width):
        keys = start + width
        mine = pl.ds(start, width)
        scores = left_product(k_ref[:, 0:keys], q_ref[:, mine])
        allowed = allowed_pairs(keys, start, width, len_ref)
        scores = jnp.where(allowed, scores, NEG)
        top = jnp.max(scores, axis=0, keepdims=True)
        expo = jnp.exp(scores - top)
        total = jnp.sum(expo, axis=0, keepdims=True)
        probs = (expo * (1.0 / total)).astype(jnp.bfloat16)
        o_ref[:, mine] = product(v_ref[:, 0:keys], probs).astype(o_ref.dtype)
        log_ref[0, :, mine] = top + jnp.log(total)


def attend_back_kernel(
    q_ref, k_ref, v_ref, go_ref, log_ref, len_ref,
    gq_ref, gk_ref, gv_ref, gk_sum, gv_sum,
):
    tokens = q_ref.shape[1]
    width = tokens // 4
    gk_sum[...] = jnp.zeros_like(gk_sum)
    gv_sum[...] = jnp.zeros_like(gv_sum)
    for start in range(0, tokens, width):
        keys = start + width
        mine = pl.ds(start, width)
        queries, upstream = q_ref[:, mine], go_ref[:, mine]
        scores = left_product(k_ref[:, 0:keys], queries)
        allowed = allowed_pairs(keys, start, width, len_ref)
        probs = jnp.exp(jnp.where(allowed, scores, NEG) - log_ref[0, :, mine])
        grad_probs = left_product(v_ref[:, 0:keys], upstream)
        inner = jnp.sum(probs * grad_probs, axis=0, keepdims=True)
        grad_scores = (probs * (grad_probs - inner)).astype(jnp.bfloat16)
        grad_q = product(k_ref[:, 0:keys], grad_scores).astype(jnp.bfloat16)
        gq_ref[:, mine] = (grad_q.astype(jnp.float32) * HEAD_DIM ** (-0.5)).astype(gq_ref.dtype)
        gk_sum[:, 0:keys] += right_product(queries, grad_scores)
        gv_sum[:, 0:keys] += right_product(upstream, probs.astype(jnp.bfloat16))
    gk_ref[...] = gk_sum[...].astype(gk_ref.dtype)
    gv_ref[...] = gv_sum[...].astype(gv_ref.dtype)


def head_spec(tokens, offset):
    return pl.BlockSpec((HEAD_DIM, tokens), lambda head: (head + offset, 0))


def len_spec():
    return pl.BlockSpec(memory_space=pltpu.SMEM)


def local_params():
    return pltpu.CompilerParams(vmem_limit_bytes=VMEM_LIMIT)


def attend(qkv, lengths):
    size, tokens = qkv.shape[0] // 3, qkv.shape[1]
    heads = size // HEAD_DIM
    log_spec = pl.BlockSpec((1, 1, tokens), lambda head: (head, 0, 0))
    return pl.pallas_call(
        attend_kernel,
        grid=(heads,),
        in_specs=[head_spec(tokens, part * heads) for part in range(3)]
        + [len_spec()],
        out_specs=[head_spec(tokens, 0), log_spec],
        out_shape=[
            jax.ShapeDtypeStruct((size, tokens), jnp.bfloat16),
            jax.ShapeDtypeStruct((heads, 1, tokens), jnp.float32),
        ],
        compiler_params=local_params(),
    )(qkv, qkv, qkv, lengths)


def attend_back(qkv, grad_mixed, log_total, lengths):
    size, tokens = qkv.shape[0] // 3, qkv.shape[1]
    heads = size // HEAD_DIM
    log_spec = pl.BlockSpec((1, 1, tokens), lambda head: (head, 0, 0))
    return pl.pallas_call(
        attend_back_kernel,
        grid=(heads,),
        in_specs=[head_spec(tokens, part * heads) for part in range(3)]
        + [head_spec(tokens, 0), log_spec, len_spec()],
        out_specs=[head_spec(tokens, 0)] * 3,
        out_shape=[jax.ShapeDtypeStruct((size, tokens), jnp.bfloat16)] * 3,
        scratch_shapes=[pltpu.VMEM((HEAD_DIM, tokens), jnp.float32)] * 2,
        compiler_params=local_params(),
    )(qkv, qkv, qkv, grad_mixed, log_total, lengths)


def fast_shards(
    layer_input,
    ln1_gain,
    ln1_bias,
    w_query,
    w_key,
    w_value,
    b_query,
    b_value,
    w_out,
    b_out,
    ln2_gain,
    ln2_bias,
    w_fc1,
    b_fc1,
    w_fc2,
    b_fc2,
    seq_lengths,
    cotangent,
):
    half, wide = jnp.bfloat16, jnp.float32
    size, tokens = layer_input.shape
    full = 4 * size
    rows, hidden_size = w_fc1.shape
    width = 4 * size + 2 * hidden_size
    scaling = HEAD_DIM ** (-0.5)
    params = jnp.stack([ln1_gain, ln1_bias, b_out, ln2_gain, ln2_bias, b_fc2], axis=1)
    stat = pltpu.VMEM((4, 8, tokens), wide)
    slots = pltpu.VMEM((3, size, tokens), half)
    stage = pltpu.VMEM((size, tokens), half)
    own_f32 = ((size, tokens), wide)
    all_half = ((full, tokens), half)
    stats_shape = ((8, tokens), wide)
    each = 3 * CHUNKS

    normed1, stats1, weights = communicate(
        enter_kernel,
        1,
        [all_half, stats_shape, ((full, full), half)],
        [stat] + sems(each, each) + row_gather_scratch(),
        layer_input,
        params,
        w_query,
        w_key,
        w_value,
        w_out.T,
    )
    w_qkv, w_up = weights[:, : 3 * size], weights[:, 3 * size :]
    qkv_bias = jnp.concatenate([b_query, jnp.zeros_like(b_query), b_value])[:, None]
    qkv_scale = jnp.where(jnp.arange(3 * size) < size, scaling, 1.0)[:, None]
    qkv = to_half((left_product(w_qkv, normed1) + qkv_bias) * qkv_scale)
    mixed, log_total = attend(qkv, seq_lengths)
    middle, normed2, grad_mlp, stats2, w_first, w_second = communicate(
        middle_kernel,
        2,
        [own_f32, all_half, all_half, stats_shape] + [((8 * rows, hidden_size), half)] * 2,
        [slots, stage, stat] + sems(each, each, each, 3) + row_gather_scratch(),
        to_half(product(w_up, mixed)),
        layer_input,
        cotangent,
        params,
        w_fc1,
        w_fc2.T,
    )
    hidden_pre = left_product(w_first, normed2) + b_fc1[:, None]
    activated, gate_pull = jax.vjp(smooth_gate, hidden_pre)
    hidden = to_half(activated)
    grad_pre = to_half(gate_pull(left_product(w_second, grad_mlp))[0])
    grad_middle, grad_branch, output, norm2_sums, sum_first, sum_second = communicate(
        turn_kernel,
        3,
        [own_f32, all_half, own_f32, ((8, size), wide)] + [((rows, hidden_size), wide)] * 2,
        [pltpu.VMEM((size, tokens), wide), slots, stage, slots, stage, stat]
        + sems(each, 3, each, each)
        + row_scatter_scratch(rows, hidden_size, half, wide),
        to_half(product(w_first, grad_pre)),
        to_half(product(w_second, hidden)),
        middle,
        cotangent,
        stats2,
        params,
        to_half(right_product(normed2, grad_pre)),
        to_half(right_product(grad_mlp, hidden)),
    )
    grad_mixed = to_half(left_product(w_up, grad_branch))
    grad_q, grad_k, grad_v = attend_back(qkv, grad_mixed, log_total, seq_lengths)
    grad_qkv = jnp.concatenate([grad_q, grad_k, grad_v], axis=0)
    grads = jnp.concatenate(
        [
            to_half(right_product(normed1, grad_qkv)),
            to_half(right_product(grad_branch, mixed)),
        ],
        axis=1,
    )

    def along(values):
        return jnp.sum(values.astype(wide), axis=1)

    vectors = jnp.concatenate(
        [
            along(grad_q)[None],
            along(grad_v)[None],
            along(to_half(grad_middle))[None],
            norm2_sums[0:2],
            along(to_half(cotangent))[None],
            along(grad_pre).reshape(hidden_size // size, size),
            jnp.zeros((6, size), wide),
        ],
        axis=0,
    )
    vectors = jnp.pad(vectors, ((0, 0), (0, 256 - size)))
    grad_input, sum_qk, sum_vo, vector_sums = communicate(
        leave_kernel,
        4,
        [own_f32] + [((rows, full // 2), wide)] * 2 + [(vectors.shape, wide)],
        [slots, stage, stat]
        + sems(3, 3)
        + [pltpu.VMEM((8,) + vectors.shape, wide)]
        + sems(7)
        + row_scatter_scratch(rows, full // 2, half, wide),
        to_half(product(w_qkv, grad_qkv)),
        layer_input,
        stats1,
        params,
        grad_middle,
        grads,
        vectors,
    )
    vector_sums = vector_sums[:, :size]
    return (
        output,
        grad_input,
        vector_sums[10],
        vector_sums[11],
        sum_qk[:, :size],
        sum_qk[:, size:],
        sum_vo[:, :size],
        vector_sums[0],
        vector_sums[1],
        sum_vo[:, size:].T,
        vector_sums[2],
        vector_sums[3],
        vector_sums[4],
        sum_first,
        vector_sums[6:10].reshape(-1),
        sum_second.T,
        vector_sums[5],
    )


def solution(mesh):
    in_specs = (
        P("col", "row"),
        P("col"),
        P("col"),
        P("row", "col"),
        P("row", "col"),
        P("row", "col"),
        P("col"),
        P("col"),
        P("col", "row"),
        P("col"),
        P("col"),
        P("col"),
        P("row", "col"),
        P("col"),
        P("col", "row"),
        P("col"),
        P("row", None),
        P("col", "row"),
    )
    out_specs = (
        P("col", "row"),
        P("col", "row"),
        P("col"),
        P("col"),
        P("row", "col"),
        P("row", "col"),
        P("row", "col"),
        P("col"),
        P("col"),
        P("col", "row"),
        P("col"),
        P("col"),
        P("col"),
        P("row", "col"),
        P("col"),
        P("col", "row"),
        P("col"),
    )
    fits = mesh.shape["col"] == 4 and mesh.shape["row"] == 8
    body = fast_shards if fits else shards
    return jax.shard_map(body, mesh=mesh, in_specs=in_specs, out_specs=out_specs, check_vma=False)
```
